512 devices in a mesh: gx: 16 (over y, core), gy: 16 (over x_lo, z), gz: 2 (over x_hi).
Axes of the slice: x: 4 (x_hi: 2, x_lo: 2; x = x_hi * 2 + x_lo), y: 8, z: 8, core: 2. Of those that a mesh axis runs over, the one named last changes fastest.
Arguments:
- initial_thermal_state: float32 [1024, 512, 256], P('gx', 'gy', 'gz'), may hold values from -6 to 6
- thermal_spread_rate: float32 [1024, 512, 256], P('gx', 'gy', 'gz'), may hold values from 0.25 to 4
- yz_skew_factor: bfloat16 [1024, 512, 256], P('gx', 'gy', 'gz'), may hold values from -1 to 1
Outputs:
- known_source_vector: float32 [1024, 512, 256], P('gx', 'gy', 'gz')
- half_step: float32 [1024, 512, 256], P('gx', 'gy', 'gz')
The draws below stay inside these ranges and needn't reach their ends.
All inputs are finite; a program needn't handle non-finite values.
Results may differ from the reference program's by a relative error of at most 0.0003.
Values sent between devices are 32-bit elements; how exact they have to be, the bound alone decides.
No kernel may reach another device: no remote copies, remote signals or barrier semaphores. Data moves between devices by JAX's collectives and lax.ppermute only.
A program may use at most 64 MiB of HBM per device.

```python
import math
import jax
import jax.numpy as jnp
from jax import lax

NODES_ALONG_X = 1024
NODES_ALONG_Y = 512
NODES_ALONG_Z = 256


def block_levels(rng, dims, split, low, largest):
    level, own = 1.0, jax.random.fold_in(rng, 6)
    for axis_at, shards_of in split:
        steps = jnp.exp(jax.random.uniform(jax.random.fold_in(own, axis_at), (shards_of,), jnp.float32, low / len(split), largest / len(split)))
        level = level * jnp.repeat(steps, dims[axis_at] // shards_of).reshape([-1 if axis == axis_at else 1 for axis in range(len(dims))])
    return level


def bell_draw(stream_key, shape, deviation, reach, shards=(), kind=jnp.bfloat16):
    array = deviation * jax.random.normal(stream_key, shape, jnp.float32)
    if shards:
        array = array * block_levels(stream_key, shape, shards, -0.22, 0.18)
    return jnp.clip(array, -reach, reach).astype(kind)


def setup_inputs(seed: int = 0) -> dict:
    splits = jax.random.split(jax.random.key(seed), 4)
    initial_thermal_state = bell_draw(splits[0], (NODES_ALONG_X, NODES_ALONG_Y, NODES_ALONG_Z), 1.0, 6.0, ((0, 16), (1, 16), (2, 2)), jnp.float32)
    thermal_spread_rate = jnp.clip(jnp.exp(math.log(4.0) - 2.7725887 * jax.random.uniform(splits[1], (NODES_ALONG_X, NODES_ALONG_Y, NODES_ALONG_Z), jnp.float32) ** block_levels(splits[1], (NODES_ALONG_X, NODES_ALONG_Y, NODES_ALONG_Z), ((0, 16), (1, 16), (2, 2)), -0.2, 0.2)), 0.25, 4.0)
    yz_skew_factor = jnp.clip(jax.random.uniform(splits[2], (NODES_ALONG_X, NODES_ALONG_Y, NODES_ALONG_Z), jnp.float32, -1.0, 1.0) * block_levels(splits[2], (NODES_ALONG_X, NODES_ALONG_Y, NODES_ALONG_Z), ((0, 16), (1, 16), (2, 2)), -0.4, 0.0), -1.0, 1.0).astype(jnp.bfloat16)
    return {"initial_thermal_state": initial_thermal_state, "thermal_spread_rate": thermal_spread_rate, "yz_skew_factor": yz_skew_factor}


ratio_x = 4096.0
ratio_y = 0.2
ratio_z = 0.2
ratio_mix = 0.25


def boundary_flux_terms(padded_heat, padded_diff, yz_skew_factor):
    centre = padded_heat[:, 1:-1, 1:-1]
    centre_diff = padded_diff[:, 1:-1, 1:-1]
    plus_y = 0.5 * (centre_diff + padded_diff[:, 2:, 1:-1])
    minus_y = 0.5 * (centre_diff + padded_diff[:, :-2, 1:-1])
    plus_z = 0.5 * (centre_diff + padded_diff[:, 1:-1, 2:])
    minus_z = 0.5 * (centre_diff + padded_diff[:, 1:-1, :-2])
    flux_y = plus_y * (padded_heat[:, 2:, 1:-1] - centre) - minus_y * (centre - padded_heat[:, :-2, 1:-1])
    flux_z = plus_z * (padded_heat[:, 1:-1, 2:] - centre) - minus_z * (centre - padded_heat[:, 1:-1, :-2])
    mixed = padded_heat[:, 2:, 2:] - padded_heat[:, 2:, :-2] - padded_heat[:, :-2, 2:] + padded_heat[:, :-2, :-2]
    return centre + ratio_y * flux_y + ratio_z * flux_z + ratio_mix * yz_skew_factor.astype(jnp.float32) * mixed


def x_bands(padded_diff):
    centre = padded_diff[1:-1]
    minus_x = 0.5 * (centre + padded_diff[:-2])
    plus_x = 0.5 * (centre + padded_diff[2:])
    return -ratio_x * minus_x, 1.0 + ratio_x * (minus_x + plus_x), -ratio_x * plus_x


def thomas_solve(lower_band, main_band, upper_band, right_side):
    def forward(state, values):
        prev_upper, prev_side = state
        low_value, main_value, up_value, side_value = values
        pivot = main_value - low_value * prev_upper
        next_upper = up_value / pivot
        next_side = (side_value - low_value * prev_side) / pivot
        return (next_upper, next_side), (next_upper, next_side)

    start = (jnp.zeros_like(main_band[0]), jnp.zeros_like(right_side[0]))
    _, (uppers, sides) = lax.scan(forward, start, (lower_band, main_band, upper_band, right_side))

    def backward(later, values):
        up_value, side_value = values
        current = side_value - up_value * later
        return current, current

    _, solved = lax.scan(backward, jnp.zeros_like(right_side[0]), (uppers, sides), reverse=True)
    return solved


def reference(initial_thermal_state, thermal_spread_rate, yz_skew_factor):
    ghost_border_layer = ((0, 0), (1, 1), (1, 1))
    known_source_vector = boundary_flux_terms(jnp.pad(initial_thermal_state, ghost_border_layer), jnp.pad(thermal_spread_rate, ghost_border_layer), yz_skew_factor)
    lower_band, main_band, upper_band = x_bands(jnp.pad(thermal_spread_rate, ((1, 1), (0, 0), (0, 0))))
    half_step = thomas_solve(lower_band, main_band, upper_band, known_source_vector)
    return known_source_vector, half_step
```

```python
import functools

import jax
import jax.numpy as jnp
from jax import lax
from jax.experimental import pallas as pl
from jax.experimental.pallas import tpu as pltpu
from jax.sharding import PartitionSpec as P

ratio_x = 4096.0
ratio_y = 0.2
ratio_z = 0.2
ratio_mix = 0.25

NI, NJ, NK = 64, 32, 128
ROWS = NI * NJ
BLOCKS = 16
PLANES = 8
F32 = jnp.float32


def call(kernel, outs, n_in, flops, moved, name):
    spec = pl.BlockSpec(memory_space=pltpu.VMEM)
    return pl.pallas_call(
        kernel,
        out_shape=[jax.ShapeDtypeStruct(shape, F32) for shape in outs],
        in_specs=[spec] * n_in,
        out_specs=[spec] * len(outs),
        compiler_params=pltpu.CompilerParams(vmem_limit_bytes=24 * 1024 * 1024),
        cost_estimate=pl.CostEstimate(flops=flops, bytes_accessed=moved, transcendentals=0),
        name=name,
    )


def lanes():
    return lax.broadcasted_iota(jnp.int32, (NJ, NK), 1)


def rows():
    return lax.broadcasted_iota(jnp.int32, (NJ, NK), 0)


def pack_kernel(u_ref, k_ref, col_ref, low_ref, high_ref):
    turn = 1 - lax.axis_index("gz")
    lane = lanes()

    def layer(i, col):
        at = pl.ds(pl.multiple_of(i * NJ, NJ), NJ)
        u = pltpu.roll(u_ref[at, :], i + turn, 1)
        k = pltpu.roll(k_ref[at, :], (i + (NI + turn)) & (NK - 1), 1)
        col = jnp.where(lane == i, u, col)
        return jnp.where(lane == i + NI, k, col)

    def some(n, col):
        for m in range(8):
            col = layer(n * 8 + m, col)
        return col

    col_ref[...] = lax.fori_loop(0, NI // 8, some, jnp.zeros((NJ, NK), F32))
    for ref, row in ((low_ref, 0), (high_ref, NJ - 1)):
        ref[0:NI, :] = u_ref[pl.ds(row, NI, stride=NJ), :]
        ref[NI : 2 * NI, :] = k_ref[pl.ds(row, NI, stride=NJ), :]


def factor_kernel(k_ref, t_ref, q_ref, r_ref, plane_ref):
    half = 0.5 * ratio_x
    zero = jnp.zeros((NJ, NK), F32)
    one = jnp.ones((NJ, NK), F32)
    first = k_ref[0:NJ, :]
    last = k_ref[ROWS - NJ : ROWS, :]
    t_ref[0:NJ, :] = zero
    q_ref[0:NJ, :] = one
    r_ref[0:NJ, :] = zero
    t_ref[ROWS - NJ : ROWS, :] = zero
    q_ref[ROWS - NJ : ROWS, :] = zero
    r_ref[ROWS - NJ : ROWS, :] = zero

    def layer(i, state):
        here, ground, left, total = state
        at = pl.ds(pl.multiple_of(i * NJ, NJ), NJ)
        after = k_ref[pl.ds(pl.multiple_of(i * NJ + NJ, NJ), NJ), :]
        link = half * (here + after)
        r = 1.0 / ((ground + left) + link)
        t = link * r
        q = left * r
        t_ref[at, :] = t
        q_ref[at, :] = q
        r_ref[at, :] = r
        return after, 1.0 + t * ground, t * left, total + q * ground

    def some(n, state):
        for m in range(2):
            state = layer(1 + n * 2 + m, state)
        return state

    second = k_ref[NJ : 2 * NJ, :]
    start = (second, one, half * (first + second), one)
    _, ground, left, total = lax.fori_loop(0, (NI - 2) // 2, some, start)
    for c, plane in enumerate((total, left, ground, first, last)):
        plane_ref[c * NJ : c * NJ + NJ, :] = plane


def source_kernel(
    u_ref, k_ref, skew_ref, col_ref, below_ref, above_ref, t_ref, q_ref, r_ref, plane_ref,
    f_ref, b_ref, send_ref,
):
    right = lax.axis_index("gz") == 0
    lane, row = lanes(), rows()
    first_lane, last_lane = lane == 0, lane == NK - 1
    first_row, last_row = row == 0, row == NJ - 1
    far_l = jnp.where(right, 0.0, 1.0).astype(F32)
    far_r = jnp.where(right, 1.0, 0.0).astype(F32)

    wide = lax.broadcasted_iota(jnp.int32, (NI, NK), 1)
    deep = lax.broadcasted_iota(jnp.int32, (NI, NK), 0)
    slope = []
    for ref in (below_ref, above_ref):
        beyond = ref[0:NI, :]
        corner = jnp.sum(
            jnp.where(wide == deep, jnp.broadcast_to(ref[2 * NI : 2 * NI + 1, :], (NI, NK)), 0.0),
            axis=1, keepdims=True,
        )
        ahead = jnp.where(wide == NK - 1, corner * far_r, pltpu.roll(beyond, NK - 1, 1))
        back = jnp.where(wide == 0, corner * far_l, pltpu.roll(beyond, 1, 1))
        slope.append(ahead - back)

    def body_with(slope_refs):
        slope_refs[0][...] = slope[0]
        slope_refs[1][...] = slope[1]

        def layer(i, state):
            col, s, total = state
            at = pl.ds(pl.multiple_of(i * NJ, NJ), NJ)
            u, k = u_ref[at, :], k_ref[at, :]
            cu = jnp.broadcast_to(col[:, 0:1], (NJ, NK))
            ck = jnp.broadcast_to(col[:, NI : NI + 1], (NJ, NK))
            u_kp = jnp.where(last_lane, cu * far_r, pltpu.roll(u, NK - 1, 1))
            u_km = jnp.where(first_lane, cu * far_l, pltpu.roll(u, 1, 1))
            k_kp = jnp.where(last_lane, ck * far_r, pltpu.roll(k, NK - 1, 1))
            k_km = jnp.where(first_lane, ck * far_l, pltpu.roll(k, 1, 1))
            d = u_kp - u_km

            def beside(x, below, above):
                below = jnp.broadcast_to(below, (NJ, NK))
                above = jnp.broadcast_to(above, (NJ, NK))
                return (
                    jnp.where(first_row, below, pltpu.roll(x, 1, 0)),
                    jnp.where(last_row, above, pltpu.roll(x, NJ - 1, 0)),
                )

            one = pl.ds(i, 1)
            two = pl.ds(NI + i, 1)
            u_jm, u_jp = beside(u, below_ref[one, :], above_ref[one, :])
            k_jm, k_jp = beside(k, below_ref[two, :], above_ref[two, :])
            d_jm, d_jp = beside(d, slope_refs[0][one, :], slope_refs[1][one, :])
            flux_y = (k + k_jp) * (u_jp - u) - (k + k_jm) * (u - u_jm)
            flux_z = (k + k_kp) * (u_kp - u) - (k + k_km) * (u - u_km)
            f = (
                u
                + (0.5 * ratio_y) * flux_y
                + (0.5 * ratio_z) * flux_z
                + ratio_mix * skew_ref[i].astype(F32) * (d_jp - d_jm)
            )
            f_ref[at, :] = f
            s = f + s
            b_ref[at, :] = r_ref[at, :] * s
            total = total + q_ref[at, :] * s
            return pltpu.roll(col, NK - 1, 1), t_ref[at, :] * s, total, s

        def some(n, state):
            col, carried, total, s = state
            for m in range(2):
                col, carried, total, s = layer(n * 2 + m, (col, carried, total))
            return col, carried, total, s

        zero = jnp.zeros((NJ, NK), F32)
        _, _, total, s = lax.fori_loop(0, NI // 2, some, (col_ref[...], zero, zero, zero))
        planes = [plane_ref[c * NJ : c * NJ + NJ, :] for c in range(5)] + [total, s]
        half = NJ // 2
        for c, plane in enumerate(planes):
            send_ref[pl.ds(2 * c, half, stride=2 * PLANES), :] = plane[0:half]
            send_ref[pl.ds(2 * c + 1, half, stride=2 * PLANES), :] = plane[half:NJ]
        for c in range(2 * len(planes), 2 * PLANES):
            send_ref[pl.ds(c, half, stride=2 * PLANES), :] = zero[0:half]

    pl.run_scoped(
        lambda a, b: body_with((a, b)), pltpu.VMEM((NI, NK), F32), pltpu.VMEM((NI, NK), F32)
    )


def separator_kernel(got_ref, out_ref):
    half = 0.5 * ratio_x

    def plane(p, c):
        at = p * 2 * PLANES + 2 * c
        return got_ref[at : at + 2, :]

    def inner(p):
        return plane(p, 1)

    def link(p):
        return half * (plane(p, 4) + plane(p + 1, 3))

    middle = BLOCKS // 2
    left, right = [], []
    ground = plane(0, 0) + half * plane(0, 3)
    side = plane(0, 5)
    ground_r = plane(BLOCKS - 1, 2) + half * plane(BLOCKS - 1, 4)
    side_r = plane(BLOCKS - 1, 6)
    for m in range(middle):
        p, o = m, BLOCKS - 1 - m
        r = 1.0 / (ground + inner(p))
        t = inner(p) * r
        left.append((side * r, t))
        ground, side = plane(p, 2) + t * ground, plane(p, 6) + t * side
        r = 1.0 / (ground_r + inner(o))
        t = inner(o) * r
        right.append((side_r * r, t))
        ground_r, side_r = plane(o, 0) + t * ground_r, plane(o, 5) + t * side_r
        if m < middle - 1:
            r = 1.0 / (ground + link(p))
            t = link(p) * r
            left.append((side * r, t))
            ground, side = plane(p + 1, 0) + t * ground, plane(p + 1, 5) + t * side
            r = 1.0 / (ground_r + link(o - 1))
            t = link(o - 1) * r
            right.append((side_r * r, t))
            ground_r, side_r = plane(o - 1, 2) + t * ground_r, plane(o - 1, 6) + t * side_r
    joint = link(middle - 1)
    r = 1.0 / (ground + joint)
    t = joint * r
    left.append((side * r, t))
    value = (side_r + t * side) / (ground_r + t * ground)
    there = value
    values_r = [there]
    for b, t in reversed(right):
        there = b + t * there
        values_r.append(there)
    here = value
    values_l = []
    for b, t in reversed(left):
        here = b + t * here
        values_l.append(here)
    values = values_l[::-1] + values_r
    for n, v in enumerate(values):
        out_ref[2 * n : 2 * n + 2, :] = v


def back_kernel(v_ref, b_ref, t_ref, q_ref, w_ref):
    half = NJ // 2
    ends = []
    for c in range(2):
        ends.append(
            jnp.concatenate(
                [v_ref[pl.ds(2 * c, half, stride=4), :], v_ref[pl.ds(2 * c + 1, half, stride=4), :]]
            )
        )
    head, tail = ends
    w_ref[ROWS - NJ : ROWS, :] = tail

    def layer(i, w):
        at = pl.ds(pl.multiple_of(i * NJ, NJ), NJ)
        w = (b_ref[at, :] + q_ref[at, :] * head) + t_ref[at, :] * w
        w_ref[at, :] = w
        return w

    def some(n, w):
        for m in range(7):
            w = layer(NI - 2 - n * 7 - m, w)
        return w

    lax.fori_loop(0, (NI - 1) // 7, some, tail)


def body(initial_thermal_state, thermal_spread_rate, yz_skew_factor):
    u = initial_thermal_state.reshape(ROWS, NK)
    k = thermal_spread_rate.reshape(ROWS, NK)
    block = ROWS * NK
    col, low, high = call(
        pack_kernel, [(NJ, NK), (2 * NI, NK), (2 * NI, NK)], 2, block, 8 * block, "pack"
    )(u, k)
    got_col = lax.ppermute(col, "gz", [(0, 1), (1, 0)])
    t, q, r, planes = call(
        factor_kernel, [(ROWS, NK)] * 3 + [(5 * NJ, NK)], 1, 20 * block, 16 * block, "factor"
    )(k)
    ends = lax.axis_size("gy") - 1
    up = jnp.concatenate([high, jnp.broadcast_to(got_col[NJ - 1 :], (8, NK))])
    down = jnp.concatenate([low, jnp.broadcast_to(got_col[:1], (8, NK))])
    below = lax.ppermute(up, "gy", [(i, i + 1) for i in range(ends)])
    above = lax.ppermute(down, "gy", [(i + 1, i) for i in range(ends)])
    f, b, send = call(
        source_kernel, [(ROWS, NK)] * 2 + [(BLOCKS * 2 * PLANES, NK)], 10,
        50 * block, 32 * block, "source",
    )(u, k, yz_skew_factor, got_col, below, above, t, q, r, planes)
    got = lax.all_to_all(send, "gx", 0, 0, tiled=True)
    (values,) = call(
        separator_kernel, [(4 * BLOCKS, NK)], 1, block, block, "separator"
    )(got)
    mine = lax.all_to_all(values, "gx", 0, 0, tiled=True)
    (w,) = call(back_kernel, [(ROWS, NK)], 4, 4 * block, 16 * block, "back")(mine, b, t, q)
    shape = initial_thermal_state.shape
    return f.reshape(shape), w.reshape(shape)


def solution(mesh):
    spec = P("gx", "gy", "gz")
    return jax.shard_map(
        body, mesh=mesh, in_specs=(spec, spec, spec), out_specs=(spec, spec), check_vma=False
    )
```

```python
import jax
import jax.numpy as jnp
from jax import lax
from jax.experimental import pallas as pl
from jax.experimental.pallas import tpu as pltpu
from jax.sharding import PartitionSpec as P

ratio_x = 4096.0
ratio_y = 0.2
ratio_z = 0.2
ratio_mix = 0.25

NI, NJ, NK = 64, 32, 128
ROWS = NI * NJ
BLOCKS = 16
PLANES = 8
F32 = jnp.float32


def call(kernel, outs, n_in, flops, moved, name):
    spec = pl.BlockSpec(memory_space=pltpu.VMEM)
    return pl.pallas_call(
        kernel,
        out_shape=[jax.ShapeDtypeStruct(shape, F32) for shape in outs],
        in_specs=[spec] * n_in,
        out_specs=[spec] * len(outs),
        compiler_params=pltpu.CompilerParams(vmem_limit_bytes=24 * 1024 * 1024),
        cost_estimate=pl.CostEstimate(flops=flops, bytes_accessed=moved, transcendentals=0),
        name=name,
    )


def lanes():
    return lax.broadcasted_iota(jnp.int32, (NJ, NK), 1)


def rows():
    return lax.broadcasted_iota(jnp.int32, (NJ, NK), 0)


def edge_kernel(u_ref, k_ref, first_ref, second_ref, sems):
    odd = lax.rem(lax.axis_index("gy"), 2)
    copies = []
    for n, (ref, row) in enumerate(((first_ref, odd * (NJ - 1)), (second_ref, (1 - odd) * (NJ - 1)))):
        for m, source in enumerate((u_ref, k_ref)):
            copies.append(
                pltpu.make_async_copy(
                    source.at[:, row, 0, :], ref.at[m * NI : m * NI + NI, :], sems.at[2 * n + m]
                )
            )
    for copy in copies:
        copy.start()
    for copy in copies:
        copy.wait()


def pack_kernel(u_ref, k_ref, skew_ref, col_ref, skew_col_ref, wide_ref):
    turn = 1 - lax.axis_index("gz")
    lane = lanes()

    def layer(i, state):
        col, skew_col = state
        at = pl.ds(pl.multiple_of(i * NJ, NJ), NJ)
        g = skew_ref[i].astype(F32)
        wide_ref[at, :] = g
        u = pltpu.roll(u_ref[at, :], i + turn, 1)
        k = pltpu.roll(k_ref[at, :], (i + (NI + turn)) & (NK - 1), 1)
        g = pltpu.roll(g, i + turn, 1)
        here = lane == i
        col = jnp.where(here, u, col)
        return jnp.where(lane == i + NI, k, col), jnp.where(here, g, skew_col)

    def some(n, state):
        for m in range(8):
            state = layer(n * 8 + m, state)
        return state

    zero = jnp.zeros((NJ, NK), F32)
    col, skew_col = lax.fori_loop(0, NI // 8, some, (zero, zero))
    col_ref[...] = col
    skew_col_ref[...] = skew_col


def factor_kernel(k_ref, t_ref, q_ref, r_ref, plane_ref):
    half = 0.5 * ratio_x
    zero = jnp.zeros((NJ, NK), F32)
    one = jnp.ones((NJ, NK), F32)
    first = k_ref[0:NJ, :]
    last = k_ref[ROWS - NJ : ROWS, :]
    t_ref[0:NJ, :] = zero
    q_ref[0:NJ, :] = one
    r_ref[0:NJ, :] = zero
    t_ref[ROWS - NJ : ROWS, :] = zero
    q_ref[ROWS - NJ : ROWS, :] = zero
    r_ref[ROWS - NJ : ROWS, :] = zero

    def layer(i, state):
        here, ground, left, total = state
        at = pl.ds(pl.multiple_of(i * NJ, NJ), NJ)
        after = k_ref[pl.ds(pl.multiple_of(i * NJ + NJ, NJ), NJ), :]
        link = half * (here + after)
        r = 1.0 / ((ground + left) + link)
        t = link * r
        q = left * r
        t_ref[at, :] = t
        q_ref[at, :] = q
        r_ref[at, :] = r
        return after, 1.0 + t * ground, t * left, total + q * ground

    def some(n, state):
        for m in range(2):
            state = layer(1 + n * 2 + m, state)
        return state

    second = k_ref[NJ : 2 * NJ, :]
    start = (second, one, half * (first + second), one)
    _, ground, left, total = lax.fori_loop(0, (NI - 2) // 2, some, start)
    for c, plane in enumerate((total, left, ground, first, last)):
        plane_ref[c * NJ : c * NJ + NJ, :] = plane


def beside(first_ref, second_ref, at):
    odd = lax.rem(lax.axis_index("gy"), 2) == 1
    first, second = first_ref[at, :], second_ref[at, :]
    return jnp.where(odd, second, first), jnp.where(odd, first, second)


def corner_kernel(first_ref, second_ref, col_ref, out_ref):
    edge = jnp.where(lax.axis_index("gz") == 0, NK - 1, 0)
    wide = lax.broadcasted_iota(jnp.int32, (NI, NK), 1)
    deep = lax.broadcasted_iota(jnp.int32, (NI, NK), 0)
    out_ref[0:NJ, :] = col_ref[...]
    out_ref[NJ : NJ + 8, :] = jnp.zeros((8, NK), F32)
    for n, beyond in enumerate(beside(first_ref, second_ref, slice(0, NI))):
        value = jnp.sum(jnp.where(wide == edge, beyond, 0.0), axis=1, keepdims=True)
        value = jnp.where(wide == deep, jnp.broadcast_to(value, (NI, NK)), 0.0)
        out_ref[NJ + n : NJ + n + 1, :] = jnp.sum(value, axis=0, keepdims=True)


def source_kernel(u_ref, k_ref, skew_ref, first_ref, second_ref, f_ref):
    lane = lax.broadcasted_iota(jnp.int32, (8, NK), 1)
    first_lane, last_lane = lane == 0, lane == NK - 1

    def slope(u):
        ahead = jnp.where(last_lane, 0.0, pltpu.roll(u, NK - 1, 1))
        back = jnp.where(first_lane, 0.0, pltpu.roll(u, 1, 1))
        return ahead, ahead - back

    def some(n, nothing):
        base = pl.multiple_of(n * (8 * NJ), 8 * NJ)
        near = pl.ds(pl.multiple_of(n * 8, 8), 8)
        deep = pl.ds(pl.multiple_of(NI + n * 8, 8), 8)
        u_below, u_above = beside(first_ref, second_ref, near)
        k_below, k_above = beside(first_ref, second_ref, deep)

        def tile(ref, j):
            return ref[pl.ds(base + j, 8, stride=NJ), :]

        u, k = tile(u_ref, 0), tile(k_ref, 0)
        _, d_before = slope(u_below)
        flux_before = (k + k_below) * (u - u_below)
        ahead, d = slope(u)
        for j in range(NJ):
            if j < NJ - 1:
                u_next, k_next = tile(u_ref, j + 1), tile(k_ref, j + 1)
            else:
                u_next, k_next = u_above, k_above
            ahead_next, d_next = slope(u_next)
            flux = (k + k_next) * (u_next - u)
            k_ahead = jnp.where(last_lane, 0.0, pltpu.roll(k, NK - 1, 1))
            across = (k + k_ahead) * (ahead - u)
            before = jnp.where(first_lane, k * u, pltpu.roll(across, 1, 1))
            f_ref[pl.ds(base + j, 8, stride=NJ), :] = (
                u
                + (0.5 * ratio_y) * (flux - flux_before)
                + (0.5 * ratio_z) * (across - before)
                + (ratio_mix * tile(skew_ref, j)) * (d_next - d_before)
            )
            u, k, ahead, flux_before, d_before, d = u_next, k_next, ahead_next, flux, d, d_next
        return nothing

    lax.fori_loop(0, NI // 8, some, 0)


def sweep_kernel(
    f0_ref, col_ref, skew_col_ref, got_ref, t_ref, q_ref, r_ref, plane_ref,
    f_ref, b_ref, send_ref,
):
    right = lax.axis_index("gz") == 0
    lane, row = lanes(), rows()
    own, far = col_ref[...], got_ref[0:NJ, :]
    own_k, far_k = pltpu.roll(own, NI, 1), pltpu.roll(far, NI, 1)
    below = jnp.broadcast_to(got_ref[NJ : NJ + 1, :], (NJ, NK))
    above = jnp.broadcast_to(got_ref[NJ + 1 : NJ + 2, :], (NJ, NK))
    up = jnp.where(row == NJ - 1, above, pltpu.roll(far, NJ - 1, 0))
    down = jnp.where(row == 0, below, pltpu.roll(far, 1, 0))
    sign = jnp.where(right, ratio_mix, -ratio_mix).astype(F32)
    extra = (0.5 * ratio_z) * (own_k * far + far_k * (far - own)) + (
        sign * skew_col_ref[...]
    ) * (up - down)
    edge = lane == jnp.where(right, NK - 1, 0)
    extra = pltpu.roll(extra, jnp.where(right, NK - 1, 0), 1)

    def layer(i, state):
        extra, s, total = state
        at = pl.ds(pl.multiple_of(i * NJ, NJ), NJ)
        f = f0_ref[at, :] + jnp.where(edge, extra, 0.0)
        f_ref[at, :] = f
        s = f + s
        b_ref[at, :] = r_ref[at, :] * s
        total = total + q_ref[at, :] * s
        return pltpu.roll(extra, NK - 1, 1), t_ref[at, :] * s, total, s

    def some(n, state):
        extra, carried, total, s = state
        for m in range(4):
            extra, carried, total, s = layer(n * 4 + m, (extra, carried, total))
        return extra, carried, total, s

    zero = jnp.zeros((NJ, NK), F32)
    _, _, total, s = lax.fori_loop(0, NI // 4, some, (extra, zero, zero, zero))
    planes = [plane_ref[c * NJ : c * NJ + NJ, :] for c in range(5)] + [total, s]
    half = NJ // 2
    for c, plane in enumerate(planes):
        send_ref[pl.ds(2 * c, half, stride=2 * PLANES), :] = plane[0:half]
        send_ref[pl.ds(2 * c + 1, half, stride=2 * PLANES), :] = plane[half:NJ]
    for c in range(2 * len(planes), 2 * PLANES):
        send_ref[pl.ds(c, half, stride=2 * PLANES), :] = zero[0:half]


def separator_kernel(got_ref, out_ref):
    half = 0.5 * ratio_x

    def plane(p, c):
        at = p * 2 * PLANES + 2 * c
        return got_ref[at : at + 2, :]

    def inner(p):
        return plane(p, 1)

    def link(p):
        return half * (plane(p, 4) + plane(p + 1, 3))

    middle = BLOCKS // 2
    left, right = [], []
    ground = plane(0, 0) + half * plane(0, 3)
    side = plane(0, 5)
    ground_r = plane(BLOCKS - 1, 2) + half * plane(BLOCKS - 1, 4)
    side_r = plane(BLOCKS - 1, 6)
    for m in range(middle):
        p, o = m, BLOCKS - 1 - m
        r = 1.0 / (ground + inner(p))
        t = inner(p) * r
        left.append((side * r, t))
        ground, side = plane(p, 2) + t * ground, plane(p, 6) + t * side
        r = 1.0 / (ground_r + inner(o))
        t = inner(o) * r
        right.append((side_r * r, t))
        ground_r, side_r = plane(o, 0) + t * ground_r, plane(o, 5) + t * side_r
        if m < middle - 1:
            r = 1.0 / (ground + link(p))
            t = link(p) * r
            left.append((side * r, t))
            ground, side = plane(p + 1, 0) + t * ground, plane(p + 1, 5) + t * side
            r = 1.0 / (ground_r + link(o - 1))
            t = link(o - 1) * r
            right.append((side_r * r, t))
            ground_r, side_r = plane(o - 1, 2) + t * ground_r, plane(o - 1, 6) + t * side_r
    joint = link(middle - 1)
    r = 1.0 / (ground + joint)
    t = joint * r
    left.append((side * r, t))
    value = (side_r + t * side) / (ground_r + t * ground)
    there = value
    values_r = [there]
    for b, t in reversed(right):
        there = b + t * there
        values_r.append(there)
    here = value
    values_l = []
    for b, t in reversed(left):
        here = b + t * here
        values_l.append(here)
    values = values_l[::-1] + values_r
    for n, v in enumerate(values):
        out_ref[2 * n : 2 * n + 2, :] = v


def back_kernel(v_ref, b_ref, t_ref, q_ref, w_ref):
    half = NJ // 2
    ends = []
    for c in range(2):
        ends.append(
            jnp.concatenate(
                [v_ref[pl.ds(2 * c, half, stride=4), :], v_ref[pl.ds(2 * c + 1, half, stride=4), :]]
            )
        )
    head, tail = ends
    w_ref[ROWS - NJ : ROWS, :] = tail

    def layer(i, w):
        at = pl.ds(pl.multiple_of(i * NJ, NJ), NJ)
        w = (b_ref[at, :] + q_ref[at, :] * head) + t_ref[at, :] * w
        w_ref[at, :] = w
        return w

    def some(n, w):
        for m in range(7):
            w = layer(NI - 2 - n * 7 - m, w)
        return w

    lax.fori_loop(0, (NI - 1) // 7, some, tail)


def body(initial_thermal_state, thermal_spread_rate, yz_skew_factor):
    u = initial_thermal_state.reshape(ROWS, NK)
    k = thermal_spread_rate.reshape(ROWS, NK)
    block = ROWS * NK
    single = (NI, NJ, 1, NK)
    anywhere = pl.BlockSpec(memory_space=pltpu.HBM)
    whole = pl.BlockSpec(memory_space=pltpu.VMEM)
    to_first, to_second = pl.pallas_call(
        edge_kernel,
        out_shape=[jax.ShapeDtypeStruct((2 * NI, NK), F32)] * 2,
        in_specs=[anywhere] * 2,
        out_specs=[whole] * 2,
        scratch_shapes=[pltpu.SemaphoreType.DMA((4,))],
        compiler_params=pltpu.CompilerParams(vmem_limit_bytes=56 * 1024 * 1024),
        cost_estimate=pl.CostEstimate(flops=0, bytes_accessed=8 * NI * NK * 4, transcendentals=0),
        name="edges",
    )(initial_thermal_state.reshape(single), thermal_spread_rate.reshape(single))
    count = lax.axis_size("gy")
    odd_pairs = [(i, i + 1) for i in range(1, count - 1, 2)]
    even_pairs = [(i, i + 1) for i in range(0, count, 2)]
    first = lax.ppermute(to_first, "gy", [r for a, b in odd_pairs for r in ((a, b), (b, a))])
    second = lax.ppermute(to_second, "gy", [r for a, b in even_pairs for r in ((a, b), (b, a))])
    col, skew_col, skew = call(
        pack_kernel, [(NJ, NK)] * 2 + [(ROWS, NK)], 3, 3 * block, 10 * block, "pack"
    )(u, k, yz_skew_factor)
    t, q, r, planes = call(
        factor_kernel, [(ROWS, NK)] * 3 + [(5 * NJ, NK)], 1, 20 * block, 16 * block, "factor"
    )(k)
    (to_half,) = call(corner_kernel, [(NJ + 8, NK)], 3, NI * NK, 0, "corner")(first, second, col)
    got_col = lax.ppermute(to_half, "gz", [(0, 1), (1, 0)])
    (f0,) = call(source_kernel, [(ROWS, NK)], 5, 40 * block, 16 * block, "source")(
        u, k, skew, first, second
    )
    f, b, send = call(
        sweep_kernel, [(ROWS, NK)] * 2 + [(BLOCKS * 2 * PLANES, NK)], 8,
        8 * block, 24 * block, "sweep",
    )(f0, col, skew_col, got_col, t, q, r, planes)
    got = lax.all_to_all(send, "gx", 0, 0, tiled=True)
    (values,) = call(
        separator_kernel, [(4 * BLOCKS, NK)], 1, block, block, "separator"
    )(got)
    mine = lax.all_to_all(values, "gx", 0, 0, tiled=True)
    (w,) = call(back_kernel, [(ROWS, NK)], 4, 4 * block, 16 * block, "back")(mine, b, t, q)
    shape = initial_thermal_state.shape
    return f.reshape(shape), w.reshape(shape)


def solution(mesh):
    spec = P("gx", "gy", "gz")
    return jax.shard_map(
        body, mesh=mesh, in_specs=(spec, spec, spec), out_specs=(spec, spec), check_vma=False
    )
```

```python
import jax
import jax.numpy as jnp
from jax import lax
from jax.experimental import pallas as pl
from jax.experimental.pallas import tpu as pltpu
from jax.sharding import PartitionSpec as P

ratio_x = 4096.0
ratio_y = 0.2
ratio_z = 0.2
ratio_mix = 0.25

NI, NJ, NK = 64, 32, 128
ROWS = NI * NJ
BLOCKS = 16
PLANES = 8
PART = 512
F32 = jnp.float32


def call(kernel, outs, n_in, flops, moved, name, leaving=False):
    spec = pl.BlockSpec(memory_space=pltpu.VMEM)
    out_specs = [spec] * len(outs)
    scratch = []
    if leaving:
        out_specs[0] = pl.BlockSpec(memory_space=pl.ANY)
        scratch = [pltpu.VMEM(outs[0], F32), pltpu.SemaphoreType.DMA((ROWS // PART,))]
    return pl.pallas_call(
        kernel,
        out_shape=[jax.ShapeDtypeStruct(shape, F32) for shape in outs],
        in_specs=[spec] * n_in,
        out_specs=out_specs,
        scratch_shapes=scratch,
        compiler_params=pltpu.CompilerParams(vmem_limit_bytes=24 * 1024 * 1024),
        cost_estimate=pl.CostEstimate(flops=flops, bytes_accessed=moved, transcendentals=0),
        name=name,
    )


def lanes():
    return lax.broadcasted_iota(jnp.int32, (NJ, NK), 1)


def rows():
    return lax.broadcasted_iota(jnp.int32, (NJ, NK), 0)


def edge_kernel(u_ref, k_ref, first_ref, second_ref, sems):
    odd = lax.rem(lax.axis_index("gy"), 2)
    copies = []
    for n, (ref, row) in enumerate(((first_ref, (1 - odd) * (NJ - 1)), (second_ref, odd * (NJ - 1)))):
        for m, source in enumerate((u_ref, k_ref)):
            copies.append(
                pltpu.make_async_copy(
                    source.at[:, row, 0, :], ref.at[m * NI : m * NI + NI, :], sems.at[2 * n + m]
                )
            )
    for copy in copies:
        copy.start()
    for copy in copies:
        copy.wait()


def pack_kernel(u_ref, k_ref, col_ref):
    turn = 1 - lax.axis_index("gz")
    lane = lanes()

    def layer(i, col):
        at = pl.ds(pl.multiple_of(i * NJ, NJ), NJ)
        u = pltpu.roll(u_ref[at, :], i + turn, 1)
        k = pltpu.roll(k_ref[at, :], (i + (NI + turn)) & (NK - 1), 1)
        col = jnp.where(lane == i, u, col)
        return jnp.where(lane == i + NI, k, col)

    def some(n, col):
        for m in range(8):
            col = layer(n * 8 + m, col)
        return col

    col_ref[...] = lax.fori_loop(0, NI // 8, some, jnp.zeros((NJ, NK), F32))


def factor_kernel(k_ref, skew_ref, t_ref, q_ref, r_ref, plane_ref, skew_col_ref, wide_ref):
    turn = 1 - lax.axis_index("gz")
    lane = lanes()

    def skew(i, col):
        g = skew_ref[i].astype(F32)
        wide_ref[pl.ds(pl.multiple_of(i * NJ, NJ), NJ), :] = g
        return jnp.where(lane == i, pltpu.roll(g, i + turn, 1), col)

    def skews(n, col):
        for m in range(8):
            col = skew(n * 8 + m, col)
        return col

    skew_col_ref[...] = lax.fori_loop(0, NI // 8, skews, jnp.zeros((NJ, NK), F32))
    half = 0.5 * ratio_x
    zero = jnp.zeros((NJ, NK), F32)
    one = jnp.ones((NJ, NK), F32)
    first = k_ref[0:NJ, :]
    last = k_ref[ROWS - NJ : ROWS, :]
    t_ref[0:NJ, :] = zero
    q_ref[0:NJ, :] = one
    r_ref[0:NJ, :] = zero
    t_ref[ROWS - NJ : ROWS, :] = zero
    q_ref[ROWS - NJ : ROWS, :] = zero
    r_ref[ROWS - NJ : ROWS, :] = zero

    def layer(i, state):
        here, ground, left, total = state
        at = pl.ds(pl.multiple_of(i * NJ, NJ), NJ)
        after = k_ref[pl.ds(pl.multiple_of(i * NJ + NJ, NJ), NJ), :]
        link = half * (here + after)
        r = 1.0 / ((ground + left) + link)
        t = link * r
        q = left * r
        t_ref[at, :] = t
        q_ref[at, :] = q
        r_ref[at, :] = r
        return after, 1.0 + t * ground, t * left, total + q * ground

    def some(n, state):
        for m in range(2):
            state = layer(1 + n * 2 + m, state)
        return state

    second = k_ref[NJ : 2 * NJ, :]
    start = (second, one, half * (first + second), one)
    _, ground, left, total = lax.fori_loop(0, (NI - 2) // 2, some, start)
    for c, plane in enumerate((total, left, ground, first, last)):
        plane_ref[c * NJ : c * NJ + NJ, :] = plane


def beside(first_ref, second_ref, at):
    odd = lax.rem(lax.axis_index("gy"), 2) == 1
    first, second = first_ref[at, :], second_ref[at, :]
    return jnp.where(odd, first, second), jnp.where(odd, second, first)


def corner_kernel(first_ref, second_ref, col_ref, out_ref):
    edge = jnp.where(lax.axis_index("gz") == 0, NK - 1, 0)
    wide = lax.broadcasted_iota(jnp.int32, (NI, NK), 1)
    deep = lax.broadcasted_iota(jnp.int32, (NI, NK), 0)
    out_ref[0:NJ, :] = col_ref[...]
    out_ref[NJ : NJ + 8, :] = jnp.zeros((8, NK), F32)
    for n, beyond in enumerate(beside(first_ref, second_ref, slice(0, NI))):
        value = jnp.sum(jnp.where(wide == edge, beyond, 0.0), axis=1, keepdims=True)
        value = jnp.where(wide == deep, jnp.broadcast_to(value, (NI, NK)), 0.0)
        out_ref[NJ + n : NJ + n + 1, :] = jnp.sum(value, axis=0, keepdims=True)


def source_kernel(u_ref, k_ref, skew_ref, first_ref, second_ref, f_ref):
    lane = lax.broadcasted_iota(jnp.int32, (8, NK), 1)
    first_lane, last_lane = lane == 0, lane == NK - 1

    def slope(u):
        ahead = jnp.where(last_lane, 0.0, pltpu.roll(u, NK - 1, 1))
        back = jnp.where(first_lane, 0.0, pltpu.roll(u, 1, 1))
        return ahead, ahead - back

    def some(n, nothing):
        base = pl.multiple_of(n * (8 * NJ), 8 * NJ)
        near = pl.ds(pl.multiple_of(n * 8, 8), 8)
        deep = pl.ds(pl.multiple_of(NI + n * 8, 8), 8)
        u_below, u_above = beside(first_ref, second_ref, near)
        k_below, k_above = beside(first_ref, second_ref, deep)

        def tile(ref, j):
            return ref[pl.ds(base + j, 8, stride=NJ), :]

        u, k = tile(u_ref, 0), tile(k_ref, 0)
        _, d_before = slope(u_below)
        flux_before = (k + k_below) * (u - u_below)
        ahead, d = slope(u)
        for j in range(NJ):
            if j < NJ - 1:
                u_next, k_next = tile(u_ref, j + 1), tile(k_ref, j + 1)
            else:
                u_next, k_next = u_above, k_above
            ahead_next, d_next = slope(u_next)
            flux = (k + k_next) * (u_next - u)
            k_ahead = jnp.where(last_lane, 0.0, pltpu.roll(k, NK - 1, 1))
            across = (k + k_ahead) * (ahead - u)
            before = jnp.where(first_lane, k * u, pltpu.roll(across, 1, 1))
            f_ref[pl.ds(base + j, 8, stride=NJ), :] = (
                u
                + (0.5 * ratio_y) * (flux - flux_before)
                + (0.5 * ratio_z) * (across - before)
                + (ratio_mix * tile(skew_ref, j)) * (d_next - d_before)
            )
            u, k, ahead, flux_before, d_before, d = u_next, k_next, ahead_next, flux, d, d_next
        return nothing

    lax.fori_loop(0, NI // 8, some, 0)


def sweep_kernel(
    f0_ref, col_ref, skew_col_ref, got_ref, t_ref, q_ref, r_ref, plane_ref,
    f_out, b_ref, send_ref, f_ref, sems,
):
    right = lax.axis_index("gz") == 0
    lane, row = lanes(), rows()
    own, far = col_ref[...], got_ref[0:NJ, :]
    own_k, far_k = pltpu.roll(own, NI, 1), pltpu.roll(far, NI, 1)
    below = jnp.broadcast_to(got_ref[NJ : NJ + 1, :], (NJ, NK))
    above = jnp.broadcast_to(got_ref[NJ + 1 : NJ + 2, :], (NJ, NK))
    up = jnp.where(row == NJ - 1, above, pltpu.roll(far, NJ - 1, 0))
    down = jnp.where(row == 0, below, pltpu.roll(far, 1, 0))
    sign = jnp.where(right, ratio_mix, -ratio_mix).astype(F32)
    extra = (0.5 * ratio_z) * (own_k * far + far_k * (far - own)) + (
        sign * skew_col_ref[...]
    ) * (up - down)
    edge = lane == jnp.where(right, NK - 1, 0)
    turn = jnp.where(right, NK - 1, NK)

    def layer(i, state):
        s, total = state
        at = pl.ds(pl.multiple_of(i * NJ, NJ), NJ)
        here = pltpu.roll(extra, (turn - i) & (NK - 1), 1)
        f = f0_ref[at, :] + jnp.where(edge, here, 0.0)
        f_ref[at, :] = f
        s = f + s
        b_ref[at, :] = r_ref[at, :] * s
        total = total + q_ref[at, :] * s
        return t_ref[at, :] * s, total, s

    def leave(n):
        at = pl.ds(pl.multiple_of(n * PART, PART), PART)
        return pltpu.make_async_copy(f_ref.at[at, :], f_out.at[at, :], sems.at[n])

    def some(n, state):
        carried, total, s = state
        for m in range(PART // NJ):
            carried, total, s = layer(n * (PART // NJ) + m, (carried, total))
        leave(n).start()
        return carried, total, s

    zero = jnp.zeros((NJ, NK), F32)
    _, total, s = lax.fori_loop(0, ROWS // PART, some, (zero, zero, zero))
    planes = [plane_ref[c * NJ : c * NJ + NJ, :] for c in range(5)] + [total, s]
    half = NJ // 2
    for c, plane in enumerate(planes):
        send_ref[pl.ds(2 * c, half, stride=2 * PLANES), :] = plane[0:half]
        send_ref[pl.ds(2 * c + 1, half, stride=2 * PLANES), :] = plane[half:NJ]
    for c in range(2 * len(planes), 2 * PLANES):
        send_ref[pl.ds(c, half, stride=2 * PLANES), :] = zero[0:half]
    for n in range(ROWS // PART):
        leave(n).wait()


def separator_kernel(got_ref, out_ref):
    half = 0.5 * ratio_x

    def plane(p, c):
        at = p * 2 * PLANES + 2 * c
        return got_ref[at : at + 2, :]

    def inner(p):
        return plane(p, 1)

    def link(p):
        return half * (plane(p, 4) + plane(p + 1, 3))

    middle = BLOCKS // 2
    left, right = [], []
    ground = plane(0, 0) + half * plane(0, 3)
    side = plane(0, 5)
    ground_r = plane(BLOCKS - 1, 2) + half * plane(BLOCKS - 1, 4)
    side_r = plane(BLOCKS - 1, 6)
    for m in range(middle):
        p, o = m, BLOCKS - 1 - m
        r = 1.0 / (ground + inner(p))
        t = inner(p) * r
        left.append((side * r, t))
        ground, side = plane(p, 2) + t * ground, plane(p, 6) + t * side
        r = 1.0 / (ground_r + inner(o))
        t = inner(o) * r
        right.append((side_r * r, t))
        ground_r, side_r = plane(o, 0) + t * ground_r, plane(o, 5) + t * side_r
        if m < middle - 1:
            r = 1.0 / (ground + link(p))
            t = link(p) * r
            left.append((side * r, t))
            ground, side = plane(p + 1, 0) + t * ground, plane(p + 1, 5) + t * side
            r = 1.0 / (ground_r + link(o - 1))
            t = link(o - 1) * r
            right.append((side_r * r, t))
            ground_r, side_r = plane(o - 1, 2) + t * ground_r, plane(o - 1, 6) + t * side_r
    joint = link(middle - 1)
    r = 1.0 / (ground + joint)
    t = joint * r
    left.append((side * r, t))
    value = (side_r + t * side) / (ground_r + t * ground)
    there = value
    values_r = [there]
    for b, t in reversed(right):
        there = b + t * there
        values_r.append(there)
    here = value
    values_l = []
    for b, t in reversed(left):
        here = b + t * here
        values_l.append(here)
    values = values_l[::-1] + values_r
    for n, v in enumerate(values):
        out_ref[2 * n : 2 * n + 2, :] = v


def back_kernel(v_ref, b_ref, t_ref, q_ref, w_out, w_ref, sems):
    half = NJ // 2
    ends = []
    for c in range(2):
        ends.append(
            jnp.concatenate(
                [v_ref[pl.ds(2 * c, half, stride=4), :], v_ref[pl.ds(2 * c + 1, half, stride=4), :]]
            )
        )
    head, tail = ends
    def layer(i, w):
        at = pl.ds(i * NJ, NJ)
        w = (b_ref[at, :] + q_ref[at, :] * head) + t_ref[at, :] * w
        w_ref[at, :] = w
        return w

    w_ref[ROWS - NJ : ROWS, :] = tail
    w = tail
    copies = []
    for n in reversed(range(ROWS // PART)):
        for i in reversed(range(n * (PART // NJ), min((n + 1) * (PART // NJ), NI - 1))):
            w = layer(i, w)
        at = pl.ds(n * PART, PART)
        copies.append(pltpu.make_async_copy(w_ref.at[at, :], w_out.at[at, :], sems.at[n]))
        copies[-1].start()
    for copy in copies:
        copy.wait()


def body(initial_thermal_state, thermal_spread_rate, yz_skew_factor):
    u = initial_thermal_state.reshape(ROWS, NK)
    k = thermal_spread_rate.reshape(ROWS, NK)
    block = ROWS * NK
    single = (NI, NJ, 1, NK)
    anywhere = pl.BlockSpec(memory_space=pltpu.HBM)
    whole = pl.BlockSpec(memory_space=pltpu.VMEM)
    to_first, to_second = pl.pallas_call(
        edge_kernel,
        out_shape=[jax.ShapeDtypeStruct((2 * NI, NK), F32)] * 2,
        in_specs=[anywhere] * 2,
        out_specs=[whole] * 2,
        scratch_shapes=[pltpu.SemaphoreType.DMA((4,))],
        compiler_params=pltpu.CompilerParams(vmem_limit_bytes=56 * 1024 * 1024),
        cost_estimate=pl.CostEstimate(flops=0, bytes_accessed=8 * NI * NK * 4, transcendentals=0),
        name="edges",
    )(initial_thermal_state.reshape(single), thermal_spread_rate.reshape(single))
    count = lax.axis_size("gy")
    odd_pairs = [(i, i + 1) for i in range(1, count - 1, 2)]
    even_pairs = [(i, i + 1) for i in range(0, count, 2)]
    first = lax.ppermute(to_first, "gy", [r for a, b in even_pairs for r in ((a, b), (b, a))])
    second = lax.ppermute(to_second, "gy", [r for a, b in odd_pairs for r in ((a, b), (b, a))])
    (col,) = call(pack_kernel, [(NJ, NK)], 2, 3 * block, 8 * block, "pack")(u, k)
    t, q, r, planes, skew_col, skew = call(
        factor_kernel, [(ROWS, NK)] * 3 + [(5 * NJ, NK), (NJ, NK), (ROWS, NK)], 2,
        20 * block, 22 * block, "factor",
    )(k, yz_skew_factor)
    (to_half,) = call(corner_kernel, [(NJ + 8, NK)], 3, NI * NK, 0, "corner")(first, second, col)
    got_col = lax.ppermute(to_half, "gz", [(0, 1), (1, 0)])
    (f0,) = call(source_kernel, [(ROWS, NK)], 5, 40 * block, 16 * block, "source")(
        u, k, skew, first, second
    )
    f, b, send = call(
        sweep_kernel, [(ROWS, NK)] * 2 + [(BLOCKS * 2 * PLANES, NK)], 8,
        8 * block, 24 * block, "sweep", True,
    )(f0, col, skew_col, got_col, t, q, r, planes)
    got = lax.all_to_all(send, "gx", 0, 0, tiled=True)
    (values,) = call(
        separator_kernel, [(4 * BLOCKS, NK)], 1, block, block, "separator"
    )(got)
    mine = lax.all_to_all(values, "gx", 0, 0, tiled=True)
    (w,) = call(back_kernel, [(ROWS, NK)], 4, 4 * block, 16 * block, "back", True)(mine, b, t, q)
    shape = initial_thermal_state.shape
    return f.reshape(shape), w.reshape(shape)


def solution(mesh):
    spec = P("gx", "gy", "gz")
    return jax.shard_map(
        body, mesh=mesh, in_specs=(spec, spec, spec), out_specs=(spec, spec), check_vma=False
    )
```

```python
import jax
import jax.numpy as jnp
from jax import lax
from jax.experimental import pallas as pl
from jax.experimental.pallas import tpu as pltpu
from jax.sharding import PartitionSpec as P

ratio_x = 4096.0
ratio_y = 0.2
ratio_z = 0.2
ratio_mix = 0.25

NI, NJ, NK = 64, 32, 128
ROWS = NI * NJ
BLOCKS = 16
PLANES = 8
PART = 512
F32 = jnp.float32


def call(kernel, outs, n_in, flops, moved, name, leaving=False):
    spec = pl.BlockSpec(memory_space=pltpu.VMEM)
    out_specs = [spec] * len(outs)
    scratch = []
    if leaving:
        out_specs[0] = pl.BlockSpec(memory_space=pl.ANY)
        scratch = [pltpu.VMEM(outs[0], F32), pltpu.SemaphoreType.DMA((ROWS // PART,))]
    return pl.pallas_call(
        kernel,
        out_shape=[jax.ShapeDtypeStruct(shape, F32) for shape in outs],
        in_specs=[spec] * n_in,
        out_specs=out_specs,
        scratch_shapes=scratch,
        compiler_params=pltpu.CompilerParams(vmem_limit_bytes=24 * 1024 * 1024),
        cost_estimate=pl.CostEstimate(flops=flops, bytes_accessed=moved, transcendentals=0),
        name=name,
    )


def lanes():
    return lax.broadcasted_iota(jnp.int32, (NJ, NK), 1)


def rows():
    return lax.broadcasted_iota(jnp.int32, (NJ, NK), 0)


def rows_to_send():
    run = lax.axis_size("gy") // 2
    place = lax.axis_index("gy")
    odd = lax.rem(place, 2) == 1
    lower = place < run
    last = place == run - 1
    ahead = (odd == lower, jnp.where(lower, jnp.logical_or(~odd, last), odd), ~odd)
    return [jnp.where(way, NJ - 1, 0) for way in ahead]


def edge_kernel(u_ref, k_ref, *refs):
    sems = refs[-1]
    copies = []
    for n, (ref, row) in enumerate(zip(refs, rows_to_send())):
        for m, source in enumerate((u_ref, k_ref)):
            copies.append(
                pltpu.make_async_copy(
                    source.at[:, row, 0, :], ref.at[m * NI : m * NI + NI, :], sems.at[2 * n + m]
                )
            )
    for copy in copies:
        copy.start()
    for copy in copies:
        copy.wait()


def pack_kernel(u_ref, k_ref, col_ref):
    turn = 1 - lax.axis_index("gz")
    lane = lanes()

    def layer(i, col):
        at = pl.ds(pl.multiple_of(i * NJ, NJ), NJ)
        u = pltpu.roll(u_ref[at, :], i + turn, 1)
        k = pltpu.roll(k_ref[at, :], (i + (NI + turn)) & (NK - 1), 1)
        col = jnp.where(lane == i, u, col)
        return jnp.where(lane == i + NI, k, col)

    def some(n, col):
        for m in range(8):
            col = layer(n * 8 + m, col)
        return col

    col_ref[...] = lax.fori_loop(0, NI // 8, some, jnp.zeros((NJ, NK), F32))


def factor_kernel(k_ref, skew_ref, t_ref, q_ref, r_ref, plane_ref, skew_col_ref, wide_ref):
    turn = 1 - lax.axis_index("gz")
    lane = lanes()

    def skew(i, col):
        g = skew_ref[i].astype(F32)
        wide_ref[pl.ds(pl.multiple_of(i * NJ, NJ), NJ), :] = g
        return jnp.where(lane == i, pltpu.roll(g, i + turn, 1), col)

    def skews(n, col):
        for m in range(8):
            col = skew(n * 8 + m, col)
        return col

    skew_col_ref[...] = lax.fori_loop(0, NI // 8, skews, jnp.zeros((NJ, NK), F32))
    half = 0.5 * ratio_x
    zero = jnp.zeros((NJ, NK), F32)
    one = jnp.ones((NJ, NK), F32)
    first = k_ref[0:NJ, :]
    last = k_ref[ROWS - NJ : ROWS, :]
    t_ref[0:NJ, :] = zero
    q_ref[0:NJ, :] = one
    r_ref[0:NJ, :] = zero
    t_ref[ROWS - NJ : ROWS, :] = zero
    q_ref[ROWS - NJ : ROWS, :] = zero
    r_ref[ROWS - NJ : ROWS, :] = zero

    def layer(i, state):
        here, ground, left, total = state
        at = pl.ds(pl.multiple_of(i * NJ, NJ), NJ)
        after = k_ref[pl.ds(pl.multiple_of(i * NJ + NJ, NJ), NJ), :]
        link = half * (here + after)
        r = 1.0 / ((ground + left) + link)
        t = link * r
        q = left * r
        t_ref[at, :] = t
        q_ref[at, :] = q
        r_ref[at, :] = r
        return after, 1.0 + t * ground, t * left, total + q * ground

    def some(n, state):
        for m in range(2):
            state = layer(1 + n * 2 + m, state)
        return state

    second = k_ref[NJ : 2 * NJ, :]
    start = (second, one, half * (first + second), one)
    _, ground, left, total = lax.fori_loop(0, (NI - 2) // 2, some, start)
    for c, plane in enumerate((total, left, ground, first, last)):
        plane_ref[c * NJ : c * NJ + NJ, :] = plane


def beside(refs, at):
    run = lax.axis_size("gy") // 2
    place = lax.axis_index("gy")
    odd = lax.rem(place, 2) == 1
    lower = place < run
    last, before = place == run - 1, place == run - 2
    first, second, third = [ref[at, :] for ref in refs]
    below = jnp.where(odd == lower, second, first)
    below = jnp.where(last, third, below)
    above = jnp.where(odd == lower, first, second)
    above = jnp.where(last, second, jnp.where(before, third, above))
    return below, above


def corner_kernel(first_ref, second_ref, third_ref, col_ref, out_ref):
    edge = jnp.where(lax.axis_index("gz") == 0, NK - 1, 0)
    wide = lax.broadcasted_iota(jnp.int32, (NI, NK), 1)
    deep = lax.broadcasted_iota(jnp.int32, (NI, NK), 0)
    out_ref[0:NJ, :] = col_ref[...]
    out_ref[NJ : NJ + 8, :] = jnp.zeros((8, NK), F32)
    for n, beyond in enumerate(beside((first_ref, second_ref, third_ref), slice(0, NI))):
        value = jnp.sum(jnp.where(wide == edge, beyond, 0.0), axis=1, keepdims=True)
        value = jnp.where(wide == deep, jnp.broadcast_to(value, (NI, NK)), 0.0)
        out_ref[NJ + n : NJ + n + 1, :] = jnp.sum(value, axis=0, keepdims=True)


def source_kernel(u_ref, k_ref, skew_ref, first_ref, second_ref, third_ref, f_ref):
    lane = lax.broadcasted_iota(jnp.int32, (8, NK), 1)
    first_lane, last_lane = lane == 0, lane == NK - 1

    def slope(u):
        ahead = jnp.where(last_lane, 0.0, pltpu.roll(u, NK - 1, 1))
        back = jnp.where(first_lane, 0.0, pltpu.roll(u, 1, 1))
        return ahead, ahead - back

    def some(n, nothing):
        base = pl.multiple_of(n * (8 * NJ), 8 * NJ)
        near = pl.ds(pl.multiple_of(n * 8, 8), 8)
        deep = pl.ds(pl.multiple_of(NI + n * 8, 8), 8)
        u_below, u_above = beside((first_ref, second_ref, third_ref), near)
        k_below, k_above = beside((first_ref, second_ref, third_ref), deep)

        def tile(ref, j):
            return ref[pl.ds(base + j, 8, stride=NJ), :]

        u, k = tile(u_ref, 0), tile(k_ref, 0)
        _, d_before = slope(u_below)
        flux_before = (k + k_below) * (u - u_below)
        ahead, d = slope(u)
        for j in range(NJ):
            if j < NJ - 1:
                u_next, k_next = tile(u_ref, j + 1), tile(k_ref, j + 1)
            else:
                u_next, k_next = u_above, k_above
            ahead_next, d_next = slope(u_next)
            flux = (k + k_next) * (u_next - u)
            k_ahead = jnp.where(last_lane, 0.0, pltpu.roll(k, NK - 1, 1))
            across = (k + k_ahead) * (ahead - u)
            before = jnp.where(first_lane, k * u, pltpu.roll(across, 1, 1))
            f_ref[pl.ds(base + j, 8, stride=NJ), :] = (
                u
                + (0.5 * ratio_y) * (flux - flux_before)
                + (0.5 * ratio_z) * (across - before)
                + (ratio_mix * tile(skew_ref, j)) * (d_next - d_before)
            )
            u, k, ahead, flux_before, d_before, d = u_next, k_next, ahead_next, flux, d, d_next
        return nothing

    lax.fori_loop(0, NI // 8, some, 0)


def sweep_kernel(
    f0_ref, col_ref, skew_col_ref, got_ref, t_ref, q_ref, r_ref, plane_ref,
    f_out, b_ref, send_ref, f_ref, sems,
):
    right = lax.axis_index("gz") == 0
    lane, row = lanes(), rows()
    own, far = col_ref[...], got_ref[0:NJ, :]
    own_k, far_k = pltpu.roll(own, NI, 1), pltpu.roll(far, NI, 1)
    below = jnp.broadcast_to(got_ref[NJ : NJ + 1, :], (NJ, NK))
    above = jnp.broadcast_to(got_ref[NJ + 1 : NJ + 2, :], (NJ, NK))
    up = jnp.where(row == NJ - 1, above, pltpu.roll(far, NJ - 1, 0))
    down = jnp.where(row == 0, below, pltpu.roll(far, 1, 0))
    sign = jnp.where(right, ratio_mix, -ratio_mix).astype(F32)
    extra = (0.5 * ratio_z) * (own_k * far + far_k * (far - own)) + (
        sign * skew_col_ref[...]
    ) * (up - down)
    edge = lane == jnp.where(right, NK - 1, 0)
    turn = jnp.where(right, NK - 1, NK)

    def layer(i, state):
        s, total = state
        at = pl.ds(pl.multiple_of(i * NJ, NJ), NJ)
        here = pltpu.roll(extra, (turn - i) & (NK - 1), 1)
        f = f0_ref[at, :] + jnp.where(edge, here, 0.0)
        f_ref[at, :] = f
        s = f + s
        b_ref[at, :] = r_ref[at, :] * s
        total = total + q_ref[at, :] * s
        return t_ref[at, :] * s, total, s

    def leave(n):
        at = pl.ds(pl.multiple_of(n * PART, PART), PART)
        return pltpu.make_async_copy(f_ref.at[at, :], f_out.at[at, :], sems.at[n])

    def some(n, state):
        carried, total, s = state
        for m in range(PART // NJ):
            carried, total, s = layer(n * (PART // NJ) + m, (carried, total))
        leave(n).start()
        return carried, total, s

    zero = jnp.zeros((NJ, NK), F32)
    _, total, s = lax.fori_loop(0, ROWS // PART, some, (zero, zero, zero))
    planes = [plane_ref[c * NJ : c * NJ + NJ, :] for c in range(5)] + [total, s]
    half = NJ // 2
    for c, plane in enumerate(planes):
        send_ref[pl.ds(2 * c, half, stride=2 * PLANES), :] = plane[0:half]
        send_ref[pl.ds(2 * c + 1, half, stride=2 * PLANES), :] = plane[half:NJ]
    for c in range(2 * len(planes), 2 * PLANES):
        send_ref[pl.ds(c, half, stride=2 * PLANES), :] = zero[0:half]
    for n in range(ROWS // PART):
        leave(n).wait()


def separator_kernel(got_ref, out_ref):
    half = 0.5 * ratio_x

    def plane(p, c):
        at = p * 2 * PLANES + 2 * c
        return got_ref[at : at + 2, :]

    def inner(p):
        return plane(p, 1)

    def link(p):
        return half * (plane(p, 4) + plane(p + 1, 3))

    middle = BLOCKS // 2
    left, right = [], []
    ground = plane(0, 0) + half * plane(0, 3)
    side = plane(0, 5)
    ground_r = plane(BLOCKS - 1, 2) + half * plane(BLOCKS - 1, 4)
    side_r = plane(BLOCKS - 1, 6)
    for m in range(middle):
        p, o = m, BLOCKS - 1 - m
        r = 1.0 / (ground + inner(p))
        t = inner(p) * r
        left.append((side * r, t))
        ground, side = plane(p, 2) + t * ground, plane(p, 6) + t * side
        r = 1.0 / (ground_r + inner(o))
        t = inner(o) * r
        right.append((side_r * r, t))
        ground_r, side_r = plane(o, 0) + t * ground_r, plane(o, 5) + t * side_r
        if m < middle - 1:
            r = 1.0 / (ground + link(p))
            t = link(p) * r
            left.append((side * r, t))
            ground, side = plane(p + 1, 0) + t * ground, plane(p + 1, 5) + t * side
            r = 1.0 / (ground_r + link(o - 1))
            t = link(o - 1) * r
            right.append((side_r * r, t))
            ground_r, side_r = plane(o - 1, 2) + t * ground_r, plane(o - 1, 6) + t * side_r
    joint = link(middle - 1)
    r = 1.0 / (ground + joint)
    t = joint * r
    left.append((side * r, t))
    value = (side_r + t * side) / (ground_r + t * ground)
    there = value
    values_r = [there]
    for b, t in reversed(right):
        there = b + t * there
        values_r.append(there)
    here = value
    values_l = []
    for b, t in reversed(left):
        here = b + t * here
        values_l.append(here)
    values = values_l[::-1] + values_r
    for n, v in enumerate(values):
        out_ref[2 * n : 2 * n + 2, :] = v


def back_kernel(v_ref, b_ref, t_ref, q_ref, w_out, w_ref, sems):
    half = NJ // 2
    ends = []
    for c in range(2):
        ends.append(
            jnp.concatenate(
                [v_ref[pl.ds(2 * c, half, stride=4), :], v_ref[pl.ds(2 * c + 1, half, stride=4), :]]
            )
        )
    head, tail = ends
    def layer(i, w):
        at = pl.ds(i * NJ, NJ)
        w = (b_ref[at, :] + q_ref[at, :] * head) + t_ref[at, :] * w
        w_ref[at, :] = w
        return w

    w_ref[ROWS - NJ : ROWS, :] = tail
    w = tail
    copies = []
    for n in reversed(range(ROWS // PART)):
        for i in reversed(range(n * (PART // NJ), min((n + 1) * (PART // NJ), NI - 1))):
            w = layer(i, w)
        at = pl.ds(n * PART, PART)
        copies.append(pltpu.make_async_copy(w_ref.at[at, :], w_out.at[at, :], sems.at[n]))
        copies[-1].start()
    for copy in copies:
        copy.wait()


def body(initial_thermal_state, thermal_spread_rate, yz_skew_factor):
    u = initial_thermal_state.reshape(ROWS, NK)
    k = thermal_spread_rate.reshape(ROWS, NK)
    block = ROWS * NK
    single = (NI, NJ, 1, NK)
    anywhere = pl.BlockSpec(memory_space=pltpu.HBM)
    whole = pl.BlockSpec(memory_space=pltpu.VMEM)
    sent = pl.pallas_call(
        edge_kernel,
        out_shape=[jax.ShapeDtypeStruct((2 * NI, NK), F32)] * 3,
        in_specs=[anywhere] * 2,
        out_specs=[whole] * 3,
        scratch_shapes=[pltpu.SemaphoreType.DMA((6,))],
        compiler_params=pltpu.CompilerParams(vmem_limit_bytes=56 * 1024 * 1024),
        cost_estimate=pl.CostEstimate(flops=0, bytes_accessed=8 * NI * NK * 4, transcendentals=0),
        name="edges",
    )(initial_thermal_state.reshape(single), thermal_spread_rate.reshape(single))
    count = lax.axis_size("gy")
    run = count // 2
    swaps = (
        [(i, i + 1) for i in (*range(1, run - 1, 2), *range(run, count, 2))],
        [(i, i + 1) for i in (*range(0, run - 2, 2), *range(run - 1, count - 1, 2))],
        [(run - 2, run - 1)],
    )
    beyond = [
        lax.ppermute(rows, "gy", [way for a, b in pairs for way in ((a, b), (b, a))])
        for rows, pairs in zip(sent, swaps)
    ]
    (col,) = call(pack_kernel, [(NJ, NK)], 2, 3 * block, 8 * block, "pack")(u, k)
    t, q, r, planes, skew_col, skew = call(
        factor_kernel, [(ROWS, NK)] * 3 + [(5 * NJ, NK), (NJ, NK), (ROWS, NK)], 2,
        20 * block, 22 * block, "factor",
    )(k, yz_skew_factor)
    (to_half,) = call(corner_kernel, [(NJ + 8, NK)], 4, NI * NK, 0, "corner")(*beyond, col)
    got_col = lax.ppermute(to_half, "gz", [(0, 1), (1, 0)])
    (f0,) = call(source_kernel, [(ROWS, NK)], 6, 40 * block, 16 * block, "source")(
        u, k, skew, *beyond
    )
    f, b, send = call(
        sweep_kernel, [(ROWS, NK)] * 2 + [(BLOCKS * 2 * PLANES, NK)], 8,
        8 * block, 24 * block, "sweep", True,
    )(f0, col, skew_col, got_col, t, q, r, planes)
    got = lax.all_to_all(send, "gx", 0, 0, tiled=True)
    (values,) = call(
        separator_kernel, [(4 * BLOCKS, NK)], 1, block, block, "separator"
    )(got)
    mine = lax.all_to_all(values, "gx", 0, 0, tiled=True)
    (w,) = call(back_kernel, [(ROWS, NK)], 4, 4 * block, 16 * block, "back", True)(mine, b, t, q)
    shape = initial_thermal_state.shape
    return f.reshape(shape), w.reshape(shape)


def solution(mesh):
    spec = P("gx", "gy", "gz")
    return jax.shard_map(
        body, mesh=mesh, in_specs=(spec, spec, spec), out_specs=(spec, spec), check_vma=False
    )
```

```python
import jax
import jax.numpy as jnp
from jax import lax
from jax.experimental import pallas as pl
from jax.experimental.pallas import tpu as pltpu
from jax.sharding import PartitionSpec as P

ratio_x = 4096.0
ratio_y = 0.2
ratio_z = 0.2
ratio_mix = 0.25

NI, NJ, NK = 64, 32, 128
ROWS = NI * NJ
BLOCKS = 16
PLANES = 8
PART = 512
PITCH = NJ + 8
F32 = jnp.float32


def call(kernel, outs, n_in, flops, moved, name, leaving=False):
    spec = pl.BlockSpec(memory_space=pltpu.VMEM)
    out_specs = [spec] * len(outs)
    scratch = []
    if leaving:
        out_specs[0] = pl.BlockSpec(memory_space=pl.ANY)
        scratch = [pltpu.VMEM(outs[0], F32), pltpu.SemaphoreType.DMA((ROWS // PART,))]
    return pl.pallas_call(
        kernel,
        out_shape=[jax.ShapeDtypeStruct(shape, F32) for shape in outs],
        in_specs=[spec] * n_in,
        out_specs=out_specs,
        scratch_shapes=scratch,
        compiler_params=pltpu.CompilerParams(vmem_limit_bytes=24 * 1024 * 1024),
        cost_estimate=pl.CostEstimate(flops=flops, bytes_accessed=moved, transcendentals=0),
        name=name,
    )


def lanes():
    return lax.broadcasted_iota(jnp.int32, (NJ, NK), 1)


def rows():
    return lax.broadcasted_iota(jnp.int32, (NJ, NK), 0)


def rows_to_send():
    run = lax.axis_size("gy") // 2
    place = lax.axis_index("gy")
    odd = lax.rem(place, 2) == 1
    lower = place < run
    last = place == run - 1
    ahead = (odd == lower, jnp.where(lower, jnp.logical_or(~odd, last), odd), ~odd)
    return [jnp.where(way, NJ - 1, 0) for way in ahead]


def edge_kernel(u_ref, k_ref, *refs):
    sems = refs[-1]
    copies = []
    for n, (ref, row) in enumerate(zip(refs, rows_to_send())):
        for m, source in enumerate((u_ref, k_ref)):
            copies.append(
                pltpu.make_async_copy(
                    source.at[:, row, 0, :], ref.at[m * NI : m * NI + NI, :], sems.at[2 * n + m]
                )
            )
    for copy in copies:
        copy.start()
    for copy in copies:
        copy.wait()


def by_eights(layer, start):
    def some(n, state):
        for m in range(8):
            state = layer(n * 8 + m, state)
        return state

    return lax.fori_loop(0, NI // 8, some, start)


def pack_kernel(u_ref, k_ref, col_ref, u_wide_ref, k_wide_ref, sum_ref):
    turn = 1 - lax.axis_index("gz")
    lane = lanes()

    def layer(i, col):
        at = pl.ds(pl.multiple_of(i * NJ, NJ), NJ)
        to = pl.ds(pl.multiple_of(i * PITCH, 8), NJ)
        u, k = u_ref[at, :], k_ref[at, :]
        u_wide_ref[to, :] = u
        k_wide_ref[to, :] = k
        sum_ref[to, :] = k + jnp.where(lane == NK - 1, 0.0, pltpu.roll(k, NK - 1, 1))
        col = jnp.where(lane == i, pltpu.roll(u, i + turn, 1), col)
        return jnp.where(lane == i + NI, pltpu.roll(k, (i + (NI + turn)) & (NK - 1), 1), col)

    col_ref[...] = by_eights(layer, jnp.zeros((NJ, NK), F32))


def skew_kernel(skew_ref, col_ref, wide_ref):
    turn = 1 - lax.axis_index("gz")
    lane = lanes()

    def layer(i, col):
        g = skew_ref[i].astype(F32)
        wide_ref[pl.ds(pl.multiple_of(i * PITCH, 8), NJ), :] = g
        return jnp.where(lane == i, pltpu.roll(g, i + turn, 1), col)

    col_ref[...] = by_eights(layer, jnp.zeros((NJ, NK), F32))


def factor_kernel(k_ref, t_ref, q_ref, r_ref, plane_ref):
    half = 0.5 * ratio_x
    zero = jnp.zeros((NJ, NK), F32)
    one = jnp.ones((NJ, NK), F32)
    first = k_ref[0:NJ, :]
    last = k_ref[ROWS - NJ : ROWS, :]
    t_ref[0:NJ, :] = zero
    q_ref[0:NJ, :] = one
    r_ref[0:NJ, :] = zero
    t_ref[ROWS - NJ : ROWS, :] = zero
    q_ref[ROWS - NJ : ROWS, :] = zero
    r_ref[ROWS - NJ : ROWS, :] = zero

    def layer(i, state):
        here, ground, left, total = state
        at = pl.ds(pl.multiple_of(i * NJ, NJ), NJ)
        after = k_ref[pl.ds(pl.multiple_of(i * NJ + NJ, NJ), NJ), :]
        link = half * (here + after)
        r = 1.0 / ((ground + left) + link)
        t = link * r
        q = left * r
        t_ref[at, :] = t
        q_ref[at, :] = q
        r_ref[at, :] = r
        return after, 1.0 + t * ground, t * left, total + q * ground

    def some(n, state):
        for m in range(2):
            state = layer(1 + n * 2 + m, state)
        return state

    second = k_ref[NJ : 2 * NJ, :]
    start = (second, one, half * (first + second), one)
    _, ground, left, total = lax.fori_loop(0, (NI - 2) // 2, some, start)
    for c, plane in enumerate((total, left, ground, first, last)):
        plane_ref[c * NJ : c * NJ + NJ, :] = plane


def beside(refs, at):
    run = lax.axis_size("gy") // 2
    place = lax.axis_index("gy")
    odd = lax.rem(place, 2) == 1
    lower = place < run
    last, before = place == run - 1, place == run - 2
    first, second, third = [ref[at, :] for ref in refs]
    below = jnp.where(odd == lower, second, first)
    below = jnp.where(last, third, below)
    above = jnp.where(odd == lower, first, second)
    above = jnp.where(last, second, jnp.where(before, third, above))
    return below, above


def corner_kernel(first_ref, second_ref, third_ref, col_ref, ready_ref, out_ref):
    edge = jnp.where(lax.axis_index("gz") == 0, NK - 1, 0)
    wide = lax.broadcasted_iota(jnp.int32, (NI, NK), 1)
    deep = lax.broadcasted_iota(jnp.int32, (NI, NK), 0)
    out_ref[0:NJ, :] = col_ref[...]
    out_ref[NJ : NJ + 8, :] = jnp.zeros((8, NK), F32)
    for n, beyond in enumerate(beside((first_ref, second_ref, third_ref), slice(0, NI))):
        value = jnp.sum(jnp.where(wide == edge, beyond, 0.0), axis=1, keepdims=True)
        value = jnp.where(wide == deep, jnp.broadcast_to(value, (NI, NK)), 0.0)
        out_ref[NJ + n : NJ + n + 1, :] = jnp.sum(value, axis=0, keepdims=True)


def source_kernel(u_ref, k_ref, sum_ref, skew_ref, first_ref, second_ref, third_ref, f_ref):
    lane = lax.broadcasted_iota(jnp.int32, (8, NK), 1)
    first_lane, last_lane = lane == 0, lane == NK - 1

    def slope(u):
        ahead = jnp.where(last_lane, 0.0, pltpu.roll(u, NK - 1, 1))
        back = jnp.where(first_lane, 0.0, pltpu.roll(u, 1, 1))
        return ahead, ahead - back

    def some(n, nothing):
        base = n * (8 * PITCH)
        near = pl.ds(pl.multiple_of(n * 8, 8), 8)
        deep = pl.ds(pl.multiple_of(NI + n * 8, 8), 8)
        u_below, u_above = beside((first_ref, second_ref, third_ref), near)
        k_below, k_above = beside((first_ref, second_ref, third_ref), deep)

        def tile(ref, j):
            return ref[pl.ds(base + j, 8, stride=PITCH), :]

        u, k = tile(u_ref, 0), tile(k_ref, 0)
        _, d_before = slope(u_below)
        flux_before = (k + k_below) * (u - u_below)
        ahead, d = slope(u)
        for j in range(NJ):
            if j < NJ - 1:
                u_next, k_next = tile(u_ref, j + 1), tile(k_ref, j + 1)
            else:
                u_next, k_next = u_above, k_above
            ahead_next, d_next = slope(u_next)
            flux = (k + k_next) * (u_next - u)
            across = tile(sum_ref, j) * (ahead - u)
            before = jnp.where(first_lane, k * u, pltpu.roll(across, 1, 1))
            f_ref[pl.ds(base + j, 8, stride=PITCH), :] = (
                u
                + (0.5 * ratio_y) * (flux - flux_before)
                + (0.5 * ratio_z) * (across - before)
                + (ratio_mix * tile(skew_ref, j)) * (d_next - d_before)
            )
            u, k, ahead, flux_before, d_before, d = u_next, k_next, ahead_next, flux, d, d_next
        return nothing

    lax.fori_loop(0, NI // 8, some, 0)


def sweep_kernel(
    f0_ref, col_ref, skew_col_ref, got_ref, t_ref, q_ref, r_ref, plane_ref,
    f_out, b_ref, send_ref, f_ref, sems,
):
    right = lax.axis_index("gz") == 0
    lane, row = lanes(), rows()
    own, far = col_ref[...], got_ref[0:NJ, :]
    own_k, far_k = pltpu.roll(own, NI, 1), pltpu.roll(far, NI, 1)
    below = jnp.broadcast_to(got_ref[NJ : NJ + 1, :], (NJ, NK))
    above = jnp.broadcast_to(got_ref[NJ + 1 : NJ + 2, :], (NJ, NK))
    up = jnp.where(row == NJ - 1, above, pltpu.roll(far, NJ - 1, 0))
    down = jnp.where(row == 0, below, pltpu.roll(far, 1, 0))
    sign = jnp.where(right, ratio_mix, -ratio_mix).astype(F32)
    extra = (0.5 * ratio_z) * (own_k * far + far_k * (far - own)) + (
        sign * skew_col_ref[...]
    ) * (up - down)
    edge = lane == jnp.where(right, NK - 1, 0)
    turn = jnp.where(right, NK - 1, NK)

    def layer(i, state):
        s, total = state
        at = pl.ds(pl.multiple_of(i * NJ, NJ), NJ)
        here = pltpu.roll(extra, (turn - i) & (NK - 1), 1)
        f = f0_ref[pl.ds(pl.multiple_of(i * PITCH, 8), NJ), :] + jnp.where(edge, here, 0.0)
        f_ref[at, :] = f
        s = f + s
        b_ref[at, :] = r_ref[at, :] * s
        total = total + q_ref[at, :] * s
        return t_ref[at, :] * s, total, s

    def leave(n):
        at = pl.ds(pl.multiple_of(n * PART, PART), PART)
        return pltpu.make_async_copy(f_ref.at[at, :], f_out.at[at, :], sems.at[n])

    def some(n, state):
        carried, total, s = state
        for m in range(PART // NJ):
            carried, total, s = layer(n * (PART // NJ) + m, (carried, total))
        leave(n).start()
        return carried, total, s

    zero = jnp.zeros((NJ, NK), F32)
    _, total, s = lax.fori_loop(0, ROWS // PART, some, (zero, zero, zero))
    planes = [plane_ref[c * NJ : c * NJ + NJ, :] for c in range(5)] + [total, s]
    half = NJ // 2
    for c, plane in enumerate(planes):
        send_ref[pl.ds(2 * c, half, stride=2 * PLANES), :] = plane[0:half]
        send_ref[pl.ds(2 * c + 1, half, stride=2 * PLANES), :] = plane[half:NJ]
    for c in range(2 * len(planes), 2 * PLANES):
        send_ref[pl.ds(c, half, stride=2 * PLANES), :] = zero[0:half]
    for n in range(ROWS // PART):
        leave(n).wait()


def separator_kernel(got_ref, out_ref):
    half = 0.5 * ratio_x

    def plane(p, c):
        at = p * 2 * PLANES + 2 * c
        return got_ref[at : at + 2, :]

    def inner(p):
        return plane(p, 1)

    def link(p):
        return half * (plane(p, 4) + plane(p + 1, 3))

    middle = BLOCKS // 2
    left, right = [], []
    ground = plane(0, 0) + half * plane(0, 3)
    side = plane(0, 5)
    ground_r = plane(BLOCKS - 1, 2) + half * plane(BLOCKS - 1, 4)
    side_r = plane(BLOCKS - 1, 6)
    for m in range(middle):
        p, o = m, BLOCKS - 1 - m
        r = 1.0 / (ground + inner(p))
        t = inner(p) * r
        left.append((side * r, t))
        ground, side = plane(p, 2) + t * ground, plane(p, 6) + t * side
        r = 1.0 / (ground_r + inner(o))
        t = inner(o) * r
        right.append((side_r * r, t))
        ground_r, side_r = plane(o, 0) + t * ground_r, plane(o, 5) + t * side_r
        if m < middle - 1:
            r = 1.0 / (ground + link(p))
            t = link(p) * r
            left.append((side * r, t))
            ground, side = plane(p + 1, 0) + t * ground, plane(p + 1, 5) + t * side
            r = 1.0 / (ground_r + link(o - 1))
            t = link(o - 1) * r
            right.append((side_r * r, t))
            ground_r, side_r = plane(o - 1, 2) + t * ground_r, plane(o - 1, 6) + t * side_r
    joint = link(middle - 1)
    r = 1.0 / (ground + joint)
    t = joint * r
    left.append((side * r, t))
    value = (side_r + t * side) / (ground_r + t * ground)
    there = value
    values_r = [there]
    for b, t in reversed(right):
        there = b + t * there
        values_r.append(there)
    here = value
    values_l = []
    for b, t in reversed(left):
        here = b + t * here
        values_l.append(here)
    values = values_l[::-1] + values_r
    for n, v in enumerate(values):
        out_ref[2 * n : 2 * n + 2, :] = v


def back_kernel(v_ref, b_ref, t_ref, q_ref, w_out, w_ref, sems):
    half = NJ // 2
    ends = []
    for c in range(2):
        ends.append(
            jnp.concatenate(
                [v_ref[pl.ds(2 * c, half, stride=4), :], v_ref[pl.ds(2 * c + 1, half, stride=4), :]]
            )
        )
    head, tail = ends
    def layer(i, w):
        at = pl.ds(i * NJ, NJ)
        w = (b_ref[at, :] + q_ref[at, :] * head) + t_ref[at, :] * w
        w_ref[at, :] = w
        return w

    w_ref[ROWS - NJ : ROWS, :] = tail
    w = tail
    copies = []
    for n in reversed(range(ROWS // PART)):
        for i in reversed(range(n * (PART // NJ), min((n + 1) * (PART // NJ), NI - 1))):
            w = layer(i, w)
        at = pl.ds(n * PART, PART)
        copies.append(pltpu.make_async_copy(w_ref.at[at, :], w_out.at[at, :], sems.at[n]))
        copies[-1].start()
    for copy in copies:
        copy.wait()


def body(initial_thermal_state, thermal_spread_rate, yz_skew_factor):
    u = initial_thermal_state.reshape(ROWS, NK)
    k = thermal_spread_rate.reshape(ROWS, NK)
    block = ROWS * NK
    single = (NI, NJ, 1, NK)
    anywhere = pl.BlockSpec(memory_space=pltpu.HBM)
    whole = pl.BlockSpec(memory_space=pltpu.VMEM)
    sent = pl.pallas_call(
        edge_kernel,
        out_shape=[jax.ShapeDtypeStruct((2 * NI, NK), F32)] * 3,
        in_specs=[anywhere] * 2,
        out_specs=[whole] * 3,
        scratch_shapes=[pltpu.SemaphoreType.DMA((6,))],
        compiler_params=pltpu.CompilerParams(vmem_limit_bytes=56 * 1024 * 1024),
        cost_estimate=pl.CostEstimate(flops=0, bytes_accessed=8 * NI * NK * 4, transcendentals=0),
        name="edges",
    )(initial_thermal_state.reshape(single), thermal_spread_rate.reshape(single))
    count = lax.axis_size("gy")
    run = count // 2
    swaps = (
        [(i, i + 1) for i in (*range(1, run - 1, 2), *range(run, count, 2))],
        [(i, i + 1) for i in (*range(0, run - 2, 2), *range(run - 1, count - 1, 2))],
        [(run - 2, run - 1)],
    )
    beyond = [
        lax.ppermute(rows, "gy", [way for a, b in pairs for way in ((a, b), (b, a))])
        for rows, pairs in zip(sent, swaps)
    ]
    spread = (NI * PITCH, NK)
    col, u_wide, k_wide, k_sum = call(
        pack_kernel, [(NJ, NK)] + [spread] * 3, 2, 6 * block, 20 * block, "pack"
    )(u, k)
    skew_col, skew = call(skew_kernel, [(NJ, NK), spread], 1, block, 6 * block, "skew")(
        yz_skew_factor
    )
    t, q, r, planes = call(
        factor_kernel, [(ROWS, NK)] * 3 + [(5 * NJ, NK)], 1, 20 * block, 16 * block, "factor"
    )(k)
    (to_half,) = call(corner_kernel, [(NJ + 8, NK)], 5, NI * NK, 0, "corner")(
        *beyond, col, skew_col
    )
    got_col = lax.ppermute(to_half, "gz", [(0, 1), (1, 0)])
    (f0,) = call(source_kernel, [spread], 7, 40 * block, 16 * block, "source")(
        u_wide, k_wide, k_sum, skew, *beyond
    )
    f, b, send = call(
        sweep_kernel, [(ROWS, NK)] * 2 + [(BLOCKS * 2 * PLANES, NK)], 8,
        8 * block, 24 * block, "sweep", True,
    )(f0, col, skew_col, got_col, t, q, r, planes)
    got = lax.all_to_all(send, "gx", 0, 0, tiled=True)
    (values,) = call(
        separator_kernel, [(4 * BLOCKS, NK)], 1, block, block, "separator"
    )(got)
    mine = lax.all_to_all(values, "gx", 0, 0, tiled=True)
    (w,) = call(back_kernel, [(ROWS, NK)], 4, 4 * block, 16 * block, "back", True)(mine, b, t, q)
    shape = initial_thermal_state.shape
    return f.reshape(shape), w.reshape(shape)


def solution(mesh):
    spec = P("gx", "gy", "gz")
    return jax.shard_map(
        body, mesh=mesh, in_specs=(spec, spec, spec), out_specs=(spec, spec), check_vma=False
    )
```

```python
import jax
import jax.numpy as jnp
from jax import lax
from jax.experimental import pallas as pl
from jax.experimental.pallas import tpu as pltpu
from jax.sharding import PartitionSpec as P

ratio_x = 4096.0
ratio_y = 0.2
ratio_z = 0.2
ratio_mix = 0.25

NI, NJ, NK = 64, 32, 128
ROWS = NI * NJ
BLOCKS = 16
PLANES = 8
PART = 512
PITCH = NJ + 8
F32 = jnp.float32


def call(kernel, outs, n_in, flops, moved, name, leaving=False):
    spec = pl.BlockSpec(memory_space=pltpu.VMEM)
    out_specs = [spec] * len(outs)
    scratch = []
    if leaving:
        out_specs[0] = pl.BlockSpec(memory_space=pl.ANY)
        scratch = [pltpu.VMEM(outs[0], F32), pltpu.SemaphoreType.DMA((ROWS // PART,))]
    return pl.pallas_call(
        kernel,
        out_shape=[jax.ShapeDtypeStruct(shape, F32) for shape in outs],
        in_specs=[spec] * n_in,
        out_specs=out_specs,
        scratch_shapes=scratch,
        compiler_params=pltpu.CompilerParams(vmem_limit_bytes=24 * 1024 * 1024),
        cost_estimate=pl.CostEstimate(flops=flops, bytes_accessed=moved, transcendentals=0),
        name=name,
    )


def lanes():
    return lax.broadcasted_iota(jnp.int32, (NJ, NK), 1)


def rows():
    return lax.broadcasted_iota(jnp.int32, (NJ, NK), 0)


def rows_to_send():
    run = lax.axis_size("gy") // 2
    place = lax.axis_index("gy")
    odd = lax.rem(place, 2) == 1
    lower = place < run
    last = place == run - 1
    ahead = (odd == lower, jnp.where(lower, jnp.logical_or(~odd, last), odd), ~odd)
    return [jnp.where(way, NJ - 1, 0) for way in ahead]


def edge_kernel(u_ref, k_ref, *refs):
    sems = refs[-1]
    copies = []
    for n, (ref, row) in enumerate(zip(refs, rows_to_send())):
        for m, source in enumerate((u_ref, k_ref)):
            copies.append(
                pltpu.make_async_copy(
                    source.at[:, row, 0, :], ref.at[m * NI : m * NI + NI, :], sems.at[2 * n + m]
                )
            )
    for copy in copies:
        copy.start()
    for copy in copies:
        copy.wait()


def by_eights(layer, start):
    def some(n, state):
        for m in range(8):
            state = layer(n * 8 + m, state)
        return state

    return lax.fori_loop(0, NI // 8, some, start)


def pack_kernel(u_ref, k_ref, col_ref, u_wide_ref, k_wide_ref, sum_ref):
    turn = 1 - lax.axis_index("gz")
    lane = lanes()

    def layer(i, col):
        at = pl.ds(pl.multiple_of(i * NJ, NJ), NJ)
        to = pl.ds(pl.multiple_of(i * PITCH, 8), NJ)
        u, k = u_ref[at, :], k_ref[at, :]
        u_wide_ref[to, :] = u
        k_wide_ref[to, :] = k
        sum_ref[to, :] = k + jnp.where(lane == NK - 1, 0.0, pltpu.roll(k, NK - 1, 1))
        col = jnp.where(lane == i, pltpu.roll(u, i + turn, 1), col)
        return jnp.where(lane == i + NI, pltpu.roll(k, (i + (NI + turn)) & (NK - 1), 1), col)

    col_ref[...] = by_eights(layer, jnp.zeros((NJ, NK), F32))


def skew_kernel(skew_ref, col_ref, wide_ref):
    turn = 1 - lax.axis_index("gz")
    lane = lanes()

    def layer(i, col):
        g = skew_ref[i].astype(F32)
        wide_ref[pl.ds(pl.multiple_of(i * PITCH, 8), NJ), :] = g
        return jnp.where(lane == i, pltpu.roll(g, i + turn, 1), col)

    col_ref[...] = by_eights(layer, jnp.zeros((NJ, NK), F32))


def factor_kernel(k_ref, t_ref, q_ref, r_ref, plane_ref):
    half = 0.5 * ratio_x
    zero = jnp.zeros((NJ, NK), F32)
    one = jnp.ones((NJ, NK), F32)
    first = k_ref[0:NJ, :]
    last = k_ref[ROWS - NJ : ROWS, :]
    t_ref[0:NJ, :] = zero
    q_ref[0:NJ, :] = one
    r_ref[0:NJ, :] = zero
    t_ref[ROWS - NJ : ROWS, :] = zero
    q_ref[ROWS - NJ : ROWS, :] = zero
    r_ref[ROWS - NJ : ROWS, :] = zero

    def layer(i, state):
        here, ground, left, total = state
        at = pl.ds(pl.multiple_of(i * NJ, NJ), NJ)
        after = k_ref[pl.ds(pl.multiple_of(i * NJ + NJ, NJ), NJ), :]
        link = half * (here + after)
        r = 1.0 / ((ground + left) + link)
        t = link * r
        q = left * r
        t_ref[at, :] = t
        q_ref[at, :] = q
        r_ref[at, :] = r
        return after, 1.0 + t * ground, t * left, total + q * ground

    def some(n, state):
        for m in range(2):
            state = layer(1 + n * 2 + m, state)
        return state

    second = k_ref[NJ : 2 * NJ, :]
    start = (second, one, half * (first + second), one)
    _, ground, left, total = lax.fori_loop(0, (NI - 2) // 2, some, start)
    for c, plane in enumerate((total, left, ground, first, last)):
        plane_ref[c * NJ : c * NJ + NJ, :] = plane


def beside(refs, at):
    run = lax.axis_size("gy") // 2
    place = lax.axis_index("gy")
    odd = lax.rem(place, 2) == 1
    lower = place < run
    last, before = place == run - 1, place == run - 2
    first, second, third = [ref[at, :] for ref in refs]
    below = jnp.where(odd == lower, second, first)
    below = jnp.where(last, third, below)
    above = jnp.where(odd == lower, first, second)
    above = jnp.where(last, second, jnp.where(before, third, above))
    return below, above


def corner_kernel(first_ref, second_ref, third_ref, col_ref, out_ref):
    edge = jnp.where(lax.axis_index("gz") == 0, NK - 1, 0)
    wide = lax.broadcasted_iota(jnp.int32, (NI, NK), 1)
    deep = lax.broadcasted_iota(jnp.int32, (NI, NK), 0)
    out_ref[0:NJ, :] = col_ref[...]
    out_ref[NJ : NJ + 8, :] = jnp.zeros((8, NK), F32)
    for n, beyond in enumerate(beside((first_ref, second_ref, third_ref), slice(0, NI))):
        value = jnp.sum(jnp.where(wide == edge, beyond, 0.0), axis=1, keepdims=True)
        value = jnp.where(wide == deep, jnp.broadcast_to(value, (NI, NK)), 0.0)
        out_ref[NJ + n : NJ + n + 1, :] = jnp.sum(value, axis=0, keepdims=True)


def source_kernel(u_ref, k_ref, sum_ref, skew_ref, first_ref, second_ref, third_ref, f_ref):
    lane = lax.broadcasted_iota(jnp.int32, (8, NK), 1)
    first_lane, last_lane = lane == 0, lane == NK - 1

    def slope(u):
        ahead = jnp.where(last_lane, 0.0, pltpu.roll(u, NK - 1, 1))
        back = jnp.where(first_lane, 0.0, pltpu.roll(u, 1, 1))
        return ahead, ahead - back

    def some(n, nothing):
        base = n * (8 * PITCH)
        near = pl.ds(pl.multiple_of(n * 8, 8), 8)
        deep = pl.ds(pl.multiple_of(NI + n * 8, 8), 8)
        u_below, u_above = beside((first_ref, second_ref, third_ref), near)
        k_below, k_above = beside((first_ref, second_ref, third_ref), deep)

        def tile(ref, j):
            return ref[pl.ds(base + j, 8, stride=PITCH), :]

        u, k = tile(u_ref, 0), tile(k_ref, 0)
        _, d_before = slope(u_below)
        flux_before = (k + k_below) * (u - u_below)
        ahead, d = slope(u)
        for j in range(NJ):
            if j < NJ - 1:
                u_next, k_next = tile(u_ref, j + 1), tile(k_ref, j + 1)
            else:
                u_next, k_next = u_above, k_above
            ahead_next, d_next = slope(u_next)
            flux = (k + k_next) * (u_next - u)
            across = tile(sum_ref, j) * (ahead - u)
            before = jnp.where(first_lane, k * u, pltpu.roll(across, 1, 1))
            f_ref[pl.ds(base + j, 8, stride=PITCH), :] = (
                u
                + (0.5 * ratio_y) * (flux - flux_before)
                + (0.5 * ratio_z) * (across - before)
                + (ratio_mix * tile(skew_ref, j)) * (d_next - d_before)
            )
            u, k, ahead, flux_before, d_before, d = u_next, k_next, ahead_next, flux, d, d_next
        return nothing

    lax.fori_loop(0, NI // 8, some, 0)


def sweep_kernel(
    f0_ref, col_ref, skew_col_ref, got_ref, t_ref, q_ref, r_ref, plane_ref,
    f_out, b_ref, send_ref, f_ref, sems,
):
    right = lax.axis_index("gz") == 0
    lane, row = lanes(), rows()
    own, far = col_ref[...], got_ref[0:NJ, :]
    own_k, far_k = pltpu.roll(own, NI, 1), pltpu.roll(far, NI, 1)
    below = jnp.broadcast_to(got_ref[NJ : NJ + 1, :], (NJ, NK))
    above = jnp.broadcast_to(got_ref[NJ + 1 : NJ + 2, :], (NJ, NK))
    up = jnp.where(row == NJ - 1, above, pltpu.roll(far, NJ - 1, 0))
    down = jnp.where(row == 0, below, pltpu.roll(far, 1, 0))
    sign = jnp.where(right, ratio_mix, -ratio_mix).astype(F32)
    extra = (0.5 * ratio_z) * (own_k * far + far_k * (far - own)) + (
        sign * skew_col_ref[...]
    ) * (up - down)
    edge = lane == jnp.where(right, NK - 1, 0)
    turn = jnp.where(right, NK - 1, NK)

    def layer(i, state):
        s, total = state
        at = pl.ds(pl.multiple_of(i * NJ, NJ), NJ)
        here = pltpu.roll(extra, (turn - i) & (NK - 1), 1)
        f = f0_ref[pl.ds(pl.multiple_of(i * PITCH, 8), NJ), :] + jnp.where(edge, here, 0.0)
        f_ref[at, :] = f
        s = f + s
        b_ref[at, :] = r_ref[at, :] * s
        total = total + q_ref[at, :] * s
        return t_ref[at, :] * s, total, s

    def leave(n):
        at = pl.ds(pl.multiple_of(n * PART, PART), PART)
        return pltpu.make_async_copy(f_ref.at[at, :], f_out.at[at, :], sems.at[n])

    def some(n, state):
        carried, total, s = state
        for m in range(PART // NJ):
            carried, total, s = layer(n * (PART // NJ) + m, (carried, total))
        leave(n).start()
        return carried, total, s

    zero = jnp.zeros((NJ, NK), F32)
    state = (zero, zero, zero)
    for n in range(ROWS // PART):
        state = some(n, state)
    _, total, s = state
    planes = [plane_ref[c * NJ : c * NJ + NJ, :] for c in range(5)] + [total, s]
    half = NJ // 2
    for c, plane in enumerate(planes):
        send_ref[pl.ds(2 * c, half, stride=2 * PLANES), :] = plane[0:half]
        send_ref[pl.ds(2 * c + 1, half, stride=2 * PLANES), :] = plane[half:NJ]
    for c in range(2 * len(planes), 2 * PLANES):
        send_ref[pl.ds(c, half, stride=2 * PLANES), :] = zero[0:half]
    for n in range(ROWS // PART):
        leave(n).wait()


def separator_kernel(got_ref, out_ref):
    half = 0.5 * ratio_x

    def plane(p, c):
        at = p * 2 * PLANES + 2 * c
        return got_ref[at : at + 2, :]

    def inner(p):
        return plane(p, 1)

    def link(p):
        return half * (plane(p, 4) + plane(p + 1, 3))

    middle = BLOCKS // 2
    left, right = [], []
    ground = plane(0, 0) + half * plane(0, 3)
    side = plane(0, 5)
    ground_r = plane(BLOCKS - 1, 2) + half * plane(BLOCKS - 1, 4)
    side_r = plane(BLOCKS - 1, 6)
    for m in range(middle):
        p, o = m, BLOCKS - 1 - m
        r = 1.0 / (ground + inner(p))
        t = inner(p) * r
        left.append((side * r, t))
        ground, side = plane(p, 2) + t * ground, plane(p, 6) + t * side
        r = 1.0 / (ground_r + inner(o))
        t = inner(o) * r
        right.append((side_r * r, t))
        ground_r, side_r = plane(o, 0) + t * ground_r, plane(o, 5) + t * side_r
        if m < middle - 1:
            r = 1.0 / (ground + link(p))
            t = link(p) * r
            left.append((side * r, t))
            ground, side = plane(p + 1, 0) + t * ground, plane(p + 1, 5) + t * side
            r = 1.0 / (ground_r + link(o - 1))
            t = link(o - 1) * r
            right.append((side_r * r, t))
            ground_r, side_r = plane(o - 1, 2) + t * ground_r, plane(o - 1, 6) + t * side_r
    joint = link(middle - 1)
    r = 1.0 / (ground + joint)
    t = joint * r
    left.append((side * r, t))
    value = (side_r + t * side) / (ground_r + t * ground)
    there = value
    values_r = [there]
    for b, t in reversed(right):
        there = b + t * there
        values_r.append(there)
    here = value
    values_l = []
    for b, t in reversed(left):
        here = b + t * here
        values_l.append(here)
    values = values_l[::-1] + values_r
    for n, v in enumerate(values):
        out_ref[2 * n : 2 * n + 2, :] = v


def back_kernel(v_ref, b_ref, t_ref, q_ref, w_out, w_ref, sems):
    half = NJ // 2
    ends = []
    for c in range(2):
        ends.append(
            jnp.concatenate(
                [v_ref[pl.ds(2 * c, half, stride=4), :], v_ref[pl.ds(2 * c + 1, half, stride=4), :]]
            )
        )
    head, tail = ends
    def layer(i, w):
        at = pl.ds(i * NJ, NJ)
        w = (b_ref[at, :] + q_ref[at, :] * head) + t_ref[at, :] * w
        w_ref[at, :] = w
        return w

    w_ref[ROWS - NJ : ROWS, :] = tail
    w = tail
    copies = []
    for n in reversed(range(ROWS // PART)):
        for i in reversed(range(n * (PART // NJ), min((n + 1) * (PART // NJ), NI - 1))):
            w = layer(i, w)
        at = pl.ds(n * PART, PART)
        copies.append(pltpu.make_async_copy(w_ref.at[at, :], w_out.at[at, :], sems.at[n]))
        copies[-1].start()
    for copy in copies:
        copy.wait()


def body(initial_thermal_state, thermal_spread_rate, yz_skew_factor):
    u = initial_thermal_state.reshape(ROWS, NK)
    k = thermal_spread_rate.reshape(ROWS, NK)
    block = ROWS * NK
    single = (NI, NJ, 1, NK)
    anywhere = pl.BlockSpec(memory_space=pltpu.HBM)
    whole = pl.BlockSpec(memory_space=pltpu.VMEM)
    sent = pl.pallas_call(
        edge_kernel,
        out_shape=[pltpu.VMEM((2 * NI, NK), F32)] * 3,
        in_specs=[anywhere] * 2,
        out_specs=[whole] * 3,
        scratch_shapes=[pltpu.SemaphoreType.DMA((6,))],
        compiler_params=pltpu.CompilerParams(vmem_limit_bytes=56 * 1024 * 1024),
        cost_estimate=pl.CostEstimate(flops=0, bytes_accessed=8 * NI * NK * 4, transcendentals=0),
        name="edges",
    )(initial_thermal_state.reshape(single), thermal_spread_rate.reshape(single))
    count = lax.axis_size("gy")
    run = count // 2
    swaps = (
        [(i, i + 1) for i in (*range(1, run - 1, 2), *range(run, count, 2))],
        [(i, i + 1) for i in (*range(0, run - 2, 2), *range(run - 1, count - 1, 2))],
        [(run - 2, run - 1)],
    )
    beyond = [
        lax.ppermute(rows, "gy", [way for a, b in pairs for way in ((a, b), (b, a))])
        for rows, pairs in zip(sent, swaps)
    ]
    spread = (NI * PITCH, NK)
    col, u_wide, k_wide, k_sum = call(
        pack_kernel, [(NJ, NK)] + [spread] * 3, 2, 6 * block, 20 * block, "pack"
    )(u, k)
    skew_col, skew = call(skew_kernel, [(NJ, NK), spread], 1, block, 6 * block, "skew")(
        yz_skew_factor
    )
    t, q, r, planes = call(
        factor_kernel, [(ROWS, NK)] * 3 + [(5 * NJ, NK)], 1, 20 * block, 16 * block, "factor"
    )(k)
    (to_half,) = call(corner_kernel, [(NJ + 8, NK)], 4, NI * NK, 0, "corner")(*beyond, col)
    got_col = lax.ppermute(to_half, "gz", [(0, 1), (1, 0)])
    (f0,) = call(source_kernel, [spread], 7, 40 * block, 16 * block, "source")(
        u_wide, k_wide, k_sum, skew, *beyond
    )
    f, b, send = call(
        sweep_kernel, [(ROWS, NK)] * 2 + [(BLOCKS * 2 * PLANES, NK)], 8,
        8 * block, 24 * block, "sweep", True,
    )(f0, col, skew_col, got_col, t, q, r, planes)
    got = lax.all_to_all(send, "gx", 0, 0, tiled=True)
    (values,) = call(
        separator_kernel, [(4 * BLOCKS, NK)], 1, block, block, "separator"
    )(got)
    mine = lax.all_to_all(values, "gx", 0, 0, tiled=True)
    (w,) = call(back_kernel, [(ROWS, NK)], 4, 4 * block, 16 * block, "back", True)(mine, b, t, q)
    shape = initial_thermal_state.shape
    return f.reshape(shape), w.reshape(shape)


def solution(mesh):
    spec = P("gx", "gy", "gz")
    return jax.shard_map(
        body, mesh=mesh, in_specs=(spec, spec, spec), out_specs=(spec, spec), check_vma=False
    )
```

```python
import jax
import jax.numpy as jnp
from jax import lax
from jax.experimental import pallas as pl
from jax.experimental.pallas import tpu as pltpu
from jax.sharding import PartitionSpec as P

ratio_x = 4096.0
ratio_y = 0.2
ratio_z = 0.2
ratio_mix = 0.25

NI, NJ, NK = 64, 32, 128
ROWS = NI * NJ
BLOCKS = 16
PLANES = 7
PART = 512
PITCH = NJ + 8
F32 = jnp.float32


def call(kernel, outs, n_in, flops, moved, name, leaving=False):
    spec = pl.BlockSpec(memory_space=pltpu.VMEM)
    out_specs = [spec] * len(outs)
    scratch = []
    if leaving:
        out_specs[0] = pl.BlockSpec(memory_space=pl.ANY)
        scratch = [pltpu.VMEM(outs[0], F32), pltpu.SemaphoreType.DMA((ROWS // PART,))]
    return pl.pallas_call(
        kernel,
        out_shape=[jax.ShapeDtypeStruct(shape, F32) for shape in outs],
        in_specs=[spec] * n_in,
        out_specs=out_specs,
        scratch_shapes=scratch,
        compiler_params=pltpu.CompilerParams(vmem_limit_bytes=24 * 1024 * 1024),
        cost_estimate=pl.CostEstimate(flops=flops, bytes_accessed=moved, transcendentals=0),
        name=name,
    )


def lanes():
    return lax.broadcasted_iota(jnp.int32, (NJ, NK), 1)


def rows():
    return lax.broadcasted_iota(jnp.int32, (NJ, NK), 0)


def rows_to_send():
    run = lax.axis_size("gy") // 2
    place = lax.axis_index("gy")
    odd = lax.rem(place, 2) == 1
    lower = place < run
    last = place == run - 1
    ahead = (odd == lower, jnp.where(lower, jnp.logical_or(~odd, last), odd), ~odd)
    return [jnp.where(way, NJ - 1, 0) for way in ahead]


def edge_kernel(u_ref, k_ref, *refs):
    sems = refs[-1]
    copies = []
    for n, (ref, row) in enumerate(zip(refs, rows_to_send())):
        for m, source in enumerate((u_ref, k_ref)):
            copies.append(
                pltpu.make_async_copy(
                    source.at[:, row, 0, :], ref.at[m * NI : m * NI + NI, :], sems.at[2 * n + m]
                )
            )
    for copy in copies:
        copy.start()
    for copy in copies:
        copy.wait()


def by_eights(layer, start):
    def some(n, state):
        for m in range(8):
            state = layer(n * 8 + m, state)
        return state

    return lax.fori_loop(0, NI // 8, some, start)


def pack_kernel(u_ref, k_ref, col_ref, u_wide_ref, k_wide_ref, sum_ref):
    turn = 1 - lax.axis_index("gz")
    lane = lanes()

    def layer(i, col):
        at = pl.ds(pl.multiple_of(i * NJ, NJ), NJ)
        to = pl.ds(pl.multiple_of(i * PITCH, 8), NJ)
        u, k = u_ref[at, :], k_ref[at, :]
        u_wide_ref[to, :] = u
        k_wide_ref[to, :] = k
        sum_ref[to, :] = k + jnp.where(lane == NK - 1, 0.0, pltpu.roll(k, NK - 1, 1))
        col = jnp.where(lane == i, pltpu.roll(u, i + turn, 1), col)
        return jnp.where(lane == i + NI, pltpu.roll(k, (i + (NI + turn)) & (NK - 1), 1), col)

    col_ref[...] = by_eights(layer, jnp.zeros((NJ, NK), F32))


def skew_kernel(skew_ref, col_ref, wide_ref):
    turn = 1 - lax.axis_index("gz")
    lane = lanes()

    def layer(i, col):
        g = skew_ref[i].astype(F32)
        wide_ref[pl.ds(pl.multiple_of(i * PITCH, 8), NJ), :] = g
        return jnp.where(lane == i, pltpu.roll(g, i + turn, 1), col)

    col_ref[...] = by_eights(layer, jnp.zeros((NJ, NK), F32))


def factor_kernel(k_ref, t_ref, q_ref, r_ref, plane_ref):
    half = 0.5 * ratio_x
    zero = jnp.zeros((NJ, NK), F32)
    one = jnp.ones((NJ, NK), F32)
    first = k_ref[0:NJ, :]
    last = k_ref[ROWS - NJ : ROWS, :]
    t_ref[0:NJ, :] = zero
    q_ref[0:NJ, :] = one
    r_ref[0:NJ, :] = zero
    t_ref[ROWS - NJ : ROWS, :] = zero
    q_ref[ROWS - NJ : ROWS, :] = zero
    r_ref[ROWS - NJ : ROWS, :] = zero

    def layer(i, state):
        here, ground, left, total = state
        at = pl.ds(pl.multiple_of(i * NJ, NJ), NJ)
        after = k_ref[pl.ds(pl.multiple_of(i * NJ + NJ, NJ), NJ), :]
        link = half * (here + after)
        r = 1.0 / ((ground + left) + link)
        t = link * r
        q = left * r
        t_ref[at, :] = t
        q_ref[at, :] = q
        r_ref[at, :] = r
        return after, 1.0 + t * ground, t * left, total + q * ground

    def some(n, state):
        for m in range(2):
            state = layer(1 + n * 2 + m, state)
        return state

    second = k_ref[NJ : 2 * NJ, :]
    start = (second, one, half * (first + second), one)
    _, ground, left, total = lax.fori_loop(0, (NI - 2) // 2, some, start)
    for c, plane in enumerate((total, left, ground, first, last)):
        plane_ref[c * NJ : c * NJ + NJ, :] = plane


def beside(refs, at):
    run = lax.axis_size("gy") // 2
    place = lax.axis_index("gy")
    odd = lax.rem(place, 2) == 1
    lower = place < run
    last, before = place == run - 1, place == run - 2
    first, second, third = [ref[at, :] for ref in refs]
    below = jnp.where(odd == lower, second, first)
    below = jnp.where(last, third, below)
    above = jnp.where(odd == lower, first, second)
    above = jnp.where(last, second, jnp.where(before, third, above))
    return below, above


def corner_kernel(first_ref, second_ref, third_ref, col_ref, out_ref):
    edge = jnp.where(lax.axis_index("gz") == 0, NK - 1, 0)
    wide = lax.broadcasted_iota(jnp.int32, (NI, NK), 1)
    deep = lax.broadcasted_iota(jnp.int32, (NI, NK), 0)
    out_ref[0:NJ, :] = col_ref[...]
    out_ref[NJ : NJ + 8, :] = jnp.zeros((8, NK), F32)
    for n, beyond in enumerate(beside((first_ref, second_ref, third_ref), slice(0, NI))):
        value = jnp.sum(jnp.where(wide == edge, beyond, 0.0), axis=1, keepdims=True)
        value = jnp.where(wide == deep, jnp.broadcast_to(value, (NI, NK)), 0.0)
        out_ref[NJ + n : NJ + n + 1, :] = jnp.sum(value, axis=0, keepdims=True)


def source_kernel(u_ref, k_ref, sum_ref, skew_ref, first_ref, second_ref, third_ref, f_ref):
    lane = lax.broadcasted_iota(jnp.int32, (8, NK), 1)
    first_lane, last_lane = lane == 0, lane == NK - 1

    def slope(u):
        ahead = jnp.where(last_lane, 0.0, pltpu.roll(u, NK - 1, 1))
        back = jnp.where(first_lane, 0.0, pltpu.roll(u, 1, 1))
        return ahead, ahead - back

    def some(n, nothing):
        base = n * (8 * PITCH)
        near = pl.ds(pl.multiple_of(n * 8, 8), 8)
        deep = pl.ds(pl.multiple_of(NI + n * 8, 8), 8)
        u_below, u_above = beside((first_ref, second_ref, third_ref), near)
        k_below, k_above = beside((first_ref, second_ref, third_ref), deep)

        def tile(ref, j):
            return ref[pl.ds(base + j, 8, stride=PITCH), :]

        u, k = tile(u_ref, 0), tile(k_ref, 0)
        _, d_before = slope(u_below)
        flux_before = (k + k_below) * (u - u_below)
        ahead, d = slope(u)
        for j in range(NJ):
            if j < NJ - 1:
                u_next, k_next = tile(u_ref, j + 1), tile(k_ref, j + 1)
            else:
                u_next, k_next = u_above, k_above
            ahead_next, d_next = slope(u_next)
            flux = (k + k_next) * (u_next - u)
            across = tile(sum_ref, j) * (ahead - u)
            before = jnp.where(first_lane, k * u, pltpu.roll(across, 1, 1))
            f_ref[pl.ds(base + j, 8, stride=PITCH), :] = (
                u
                + (0.5 * ratio_y) * (flux - flux_before)
                + (0.5 * ratio_z) * (across - before)
                + (ratio_mix * tile(skew_ref, j)) * (d_next - d_before)
            )
            u, k, ahead, flux_before, d_before, d = u_next, k_next, ahead_next, flux, d, d_next
        return nothing

    lax.fori_loop(0, NI // 8, some, 0)


def sweep_kernel(
    f0_ref, col_ref, skew_col_ref, got_ref, t_ref, q_ref, r_ref, plane_ref,
    f_out, b_ref, send_ref, f_ref, sems,
):
    right = lax.axis_index("gz") == 0
    lane, row = lanes(), rows()
    own, far = col_ref[...], got_ref[0:NJ, :]
    own_k, far_k = pltpu.roll(own, NI, 1), pltpu.roll(far, NI, 1)
    below = jnp.broadcast_to(got_ref[NJ : NJ + 1, :], (NJ, NK))
    above = jnp.broadcast_to(got_ref[NJ + 1 : NJ + 2, :], (NJ, NK))
    up = jnp.where(row == NJ - 1, above, pltpu.roll(far, NJ - 1, 0))
    down = jnp.where(row == 0, below, pltpu.roll(far, 1, 0))
    sign = jnp.where(right, ratio_mix, -ratio_mix).astype(F32)
    extra = (0.5 * ratio_z) * (own_k * far + far_k * (far - own)) + (
        sign * skew_col_ref[...]
    ) * (up - down)
    edge = lane == jnp.where(right, NK - 1, 0)
    turn = jnp.where(right, NK - 1, NK)

    def layer(i, state):
        s, total = state
        at = pl.ds(pl.multiple_of(i * NJ, NJ), NJ)
        here = pltpu.roll(extra, (turn - i) & (NK - 1), 1)
        f = f0_ref[pl.ds(pl.multiple_of(i * PITCH, 8), NJ), :] + jnp.where(edge, here, 0.0)
        f_ref[at, :] = f
        s = f + s
        b_ref[at, :] = r_ref[at, :] * s
        total = total + q_ref[at, :] * s
        return t_ref[at, :] * s, total, s

    def leave(n):
        at = pl.ds(pl.multiple_of(n * PART, PART), PART)
        return pltpu.make_async_copy(f_ref.at[at, :], f_out.at[at, :], sems.at[n])

    def some(n, state):
        carried, total, s = state
        for m in range(PART // NJ):
            carried, total, s = layer(n * (PART // NJ) + m, (carried, total))
        leave(n).start()
        return carried, total, s

    zero = jnp.zeros((NJ, NK), F32)
    state = (zero, zero, zero)
    for n in range(ROWS // PART):
        state = some(n, state)
    _, total, s = state
    planes = [plane_ref[c * NJ : c * NJ + NJ, :] for c in range(5)] + [total, s]
    for c, plane in enumerate(planes):
        for q in range(BLOCKS):
            send_ref[q, :, c * NK : c * NK + NK] = plane[2 * q : 2 * q + 2]
    for n in range(ROWS // PART):
        leave(n).wait()


def separator_kernel(got_ref, out_ref):
    half = 0.5 * ratio_x

    def plane(p, c):
        return got_ref[p, :, c * NK : c * NK + NK]

    def inner(p):
        return plane(p, 1)

    def link(p):
        return half * (plane(p, 4) + plane(p + 1, 3))

    middle = BLOCKS // 2
    left, right = [], []
    ground = plane(0, 0) + half * plane(0, 3)
    side = plane(0, 5)
    ground_r = plane(BLOCKS - 1, 2) + half * plane(BLOCKS - 1, 4)
    side_r = plane(BLOCKS - 1, 6)
    for m in range(middle):
        p, o = m, BLOCKS - 1 - m
        r = 1.0 / (ground + inner(p))
        t = inner(p) * r
        left.append((side * r, t))
        ground, side = plane(p, 2) + t * ground, plane(p, 6) + t * side
        r = 1.0 / (ground_r + inner(o))
        t = inner(o) * r
        right.append((side_r * r, t))
        ground_r, side_r = plane(o, 0) + t * ground_r, plane(o, 5) + t * side_r
        if m < middle - 1:
            r = 1.0 / (ground + link(p))
            t = link(p) * r
            left.append((side * r, t))
            ground, side = plane(p + 1, 0) + t * ground, plane(p + 1, 5) + t * side
            r = 1.0 / (ground_r + link(o - 1))
            t = link(o - 1) * r
            right.append((side_r * r, t))
            ground_r, side_r = plane(o - 1, 2) + t * ground_r, plane(o - 1, 6) + t * side_r
    joint = link(middle - 1)
    r = 1.0 / (ground + joint)
    t = joint * r
    left.append((side * r, t))
    value = (side_r + t * side) / (ground_r + t * ground)
    there = value
    values_r = [there]
    for b, t in reversed(right):
        there = b + t * there
        values_r.append(there)
    here = value
    values_l = []
    for b, t in reversed(left):
        here = b + t * here
        values_l.append(here)
    values = values_l[::-1] + values_r
    for n, v in enumerate(values):
        out_ref[2 * n : 2 * n + 2, :] = v


def back_kernel(v_ref, b_ref, t_ref, q_ref, w_out, w_ref, sems):
    half = NJ // 2
    for c in range(4):
        w_ref[pl.ds(c // 2 * NJ + c % 2, half, stride=2), :] = v_ref[pl.ds(c, half, stride=4), :]
    head, tail = w_ref[0:NJ, :], w_ref[NJ : 2 * NJ, :]

    def layer(i, w):
        at = pl.ds(i * NJ, NJ)
        w = (b_ref[at, :] + q_ref[at, :] * head) + t_ref[at, :] * w
        w_ref[at, :] = w
        return w

    w_ref[ROWS - NJ : ROWS, :] = tail
    w = tail
    copies = []
    for n in reversed(range(ROWS // PART)):
        for i in reversed(range(n * (PART // NJ), min((n + 1) * (PART // NJ), NI - 1))):
            w = layer(i, w)
        at = pl.ds(n * PART, PART)
        copies.append(pltpu.make_async_copy(w_ref.at[at, :], w_out.at[at, :], sems.at[n]))
        copies[-1].start()
    for copy in copies:
        copy.wait()


def body(initial_thermal_state, thermal_spread_rate, yz_skew_factor):
    u = initial_thermal_state.reshape(ROWS, NK)
    k = thermal_spread_rate.reshape(ROWS, NK)
    block = ROWS * NK
    single = (NI, NJ, 1, NK)
    anywhere = pl.BlockSpec(memory_space=pltpu.HBM)
    whole = pl.BlockSpec(memory_space=pltpu.VMEM)
    sent = pl.pallas_call(
        edge_kernel,
        out_shape=[pltpu.VMEM((2 * NI, NK), F32)] * 3,
        in_specs=[anywhere] * 2,
        out_specs=[whole] * 3,
        scratch_shapes=[pltpu.SemaphoreType.DMA((6,))],
        compiler_params=pltpu.CompilerParams(vmem_limit_bytes=56 * 1024 * 1024),
        cost_estimate=pl.CostEstimate(flops=0, bytes_accessed=8 * NI * NK * 4, transcendentals=0),
        name="edges",
    )(initial_thermal_state.reshape(single), thermal_spread_rate.reshape(single))
    count = lax.axis_size("gy")
    run = count // 2
    swaps = (
        [(i, i + 1) for i in (*range(1, run - 1, 2), *range(run, count, 2))],
        [(i, i + 1) for i in (*range(0, run - 2, 2), *range(run - 1, count - 1, 2))],
        [(run - 2, run - 1)],
    )
    beyond = [
        lax.ppermute(rows, "gy", [way for a, b in pairs for way in ((a, b), (b, a))])
        for rows, pairs in zip(sent, swaps)
    ]
    spread = (NI * PITCH, NK)
    col, u_wide, k_wide, k_sum = call(
        pack_kernel, [(NJ, NK)] + [spread] * 3, 2, 6 * block, 20 * block, "pack"
    )(u, k)
    skew_col, skew = call(skew_kernel, [(NJ, NK), spread], 1, block, 6 * block, "skew")(
        yz_skew_factor
    )
    t, q, r, planes = call(
        factor_kernel, [(ROWS, NK)] * 3 + [(5 * NJ, NK)], 1, 20 * block, 16 * block, "factor"
    )(k)
    (to_half,) = call(corner_kernel, [(NJ + 8, NK)], 4, NI * NK, 0, "corner")(*beyond, col)
    got_col = lax.ppermute(to_half, "gz", [(0, 1), (1, 0)])
    (f0,) = call(source_kernel, [spread], 7, 40 * block, 16 * block, "source")(
        u_wide, k_wide, k_sum, skew, *beyond
    )
    f, b, send = call(
        sweep_kernel, [(ROWS, NK)] * 2 + [(BLOCKS, 2, PLANES * NK)], 8,
        8 * block, 24 * block, "sweep", True,
    )(f0, col, skew_col, got_col, t, q, r, planes)
    got = lax.all_to_all(send, "gx", 0, 0, tiled=True)
    (values,) = call(
        separator_kernel, [(4 * BLOCKS, NK)], 1, block, block, "separator"
    )(got)
    mine = lax.all_to_all(values, "gx", 0, 0, tiled=True)
    (w,) = call(back_kernel, [(ROWS, NK)], 4, 4 * block, 16 * block, "back", True)(mine, b, t, q)
    shape = initial_thermal_state.shape
    return f.reshape(shape), w.reshape(shape)


def solution(mesh):
    spec = P("gx", "gy", "gz")
    return jax.shard_map(
        body, mesh=mesh, in_specs=(spec, spec, spec), out_specs=(spec, spec), check_vma=False
    )
```

```python
import jax
import jax.numpy as jnp
from jax import lax
from jax.experimental import pallas as pl
from jax.experimental.pallas import tpu as pltpu
from jax.sharding import PartitionSpec as P

ratio_x = 4096.0
ratio_y = 0.2
ratio_z = 0.2
ratio_mix = 0.25

NI, NJ, NK = 64, 32, 128
ROWS = NI * NJ
BLOCKS = 16
PLANES = 7
PART = 512
PITCH = NJ + 8
F32 = jnp.float32


def call(kernel, outs, n_in, flops, moved, name, leaving=False):
    spec = pl.BlockSpec(memory_space=pltpu.VMEM)
    out_specs = [spec] * len(outs)
    scratch = []
    if leaving:
        out_specs[0] = pl.BlockSpec(memory_space=pl.ANY)
        scratch = [pltpu.VMEM(outs[0], F32), pltpu.SemaphoreType.DMA((ROWS // PART,))]
    return pl.pallas_call(
        kernel,
        out_shape=[jax.ShapeDtypeStruct(shape, F32) for shape in outs],
        in_specs=[spec] * n_in,
        out_specs=out_specs,
        scratch_shapes=scratch,
        compiler_params=pltpu.CompilerParams(vmem_limit_bytes=24 * 1024 * 1024),
        cost_estimate=pl.CostEstimate(flops=flops, bytes_accessed=moved, transcendentals=0),
        name=name,
    )


def lanes():
    return lax.broadcasted_iota(jnp.int32, (NJ, NK), 1)


def rows():
    return lax.broadcasted_iota(jnp.int32, (NJ, NK), 0)


def rows_to_send():
    run = lax.axis_size("gy") // 2
    place = lax.axis_index("gy")
    odd = lax.rem(place, 2) == 1
    lower = place < run
    last = place == run - 1
    ahead = (odd == lower, jnp.where(lower, jnp.logical_or(~odd, last), odd), ~odd)
    return [jnp.where(way, NJ - 1, 0) for way in ahead]


def edge_kernel(u_ref, k_ref, *refs):
    sems = refs[-1]
    copies = []
    for n, (ref, row) in enumerate(zip(refs, rows_to_send())):
        for m, source in enumerate((u_ref, k_ref)):
            copies.append(
                pltpu.make_async_copy(
                    source.at[:, row, 0, :], ref.at[m * NI : m * NI + NI, :], sems.at[2 * n + m]
                )
            )
    for copy in copies:
        copy.start()
    for copy in copies:
        copy.wait()


def by_eights(layer, start):
    def some(n, state):
        for m in range(8):
            state = layer(n * 8 + m, state)
        return state

    return lax.fori_loop(0, NI // 8, some, start)


def pack_kernel(u_ref, k_ref, col_ref, u_wide_ref, k_wide_ref, sum_ref):
    turn = 1 - lax.axis_index("gz")
    lane = lanes()

    def layer(i, col):
        at = pl.ds(pl.multiple_of(i * NJ, NJ), NJ)
        to = pl.ds(pl.multiple_of(i * PITCH, 8), NJ)
        u, k = u_ref[at, :], k_ref[at, :]
        u_wide_ref[to, :] = u
        k_wide_ref[to, :] = k
        sum_ref[to, :] = k + jnp.where(lane == NK - 1, 0.0, pltpu.roll(k, NK - 1, 1))
        col = jnp.where(lane == i, pltpu.roll(u, i + turn, 1), col)
        return jnp.where(lane == i + NI, pltpu.roll(k, (i + (NI + turn)) & (NK - 1), 1), col)

    col_ref[...] = by_eights(layer, jnp.zeros((NJ, NK), F32))


def factor_kernel(k_ref, skew_ref, t_ref, q_ref, r_ref, plane_ref, wide_ref):
    def widen(i):
        wide_ref[pl.ds(pl.multiple_of(i * PITCH, 8), NJ), :] = skew_ref[i].astype(F32)

    widen(0)
    widen(NI - 1)
    half = 0.5 * ratio_x
    zero = jnp.zeros((NJ, NK), F32)
    one = jnp.ones((NJ, NK), F32)
    first = k_ref[0:NJ, :]
    last = k_ref[ROWS - NJ : ROWS, :]
    t_ref[0:NJ, :] = zero
    q_ref[0:NJ, :] = one
    r_ref[0:NJ, :] = zero
    t_ref[ROWS - NJ : ROWS, :] = zero
    q_ref[ROWS - NJ : ROWS, :] = zero
    r_ref[ROWS - NJ : ROWS, :] = zero

    def layer(i, state):
        here, ground, left, total = state
        widen(i)
        at = pl.ds(pl.multiple_of(i * NJ, NJ), NJ)
        after = k_ref[pl.ds(pl.multiple_of(i * NJ + NJ, NJ), NJ), :]
        link = half * (here + after)
        r = 1.0 / ((ground + left) + link)
        t = link * r
        q = left * r
        t_ref[at, :] = t
        q_ref[at, :] = q
        r_ref[at, :] = r
        return after, 1.0 + t * ground, t * left, total + q * ground

    def some(n, state):
        for m in range(2):
            state = layer(1 + n * 2 + m, state)
        return state

    second = k_ref[NJ : 2 * NJ, :]
    start = (second, one, half * (first + second), one)
    _, ground, left, total = lax.fori_loop(0, (NI - 2) // 2, some, start)
    for c, plane in enumerate((total, left, ground, first, last)):
        plane_ref[c * NJ : c * NJ + NJ, :] = plane


def beside(refs, at):
    run = lax.axis_size("gy") // 2
    place = lax.axis_index("gy")
    odd = lax.rem(place, 2) == 1
    lower = place < run
    last, before = place == run - 1, place == run - 2
    first, second, third = [ref[at, :] for ref in refs]
    below = jnp.where(odd == lower, second, first)
    below = jnp.where(last, third, below)
    above = jnp.where(odd == lower, first, second)
    above = jnp.where(last, second, jnp.where(before, third, above))
    return below, above


def corner_kernel(first_ref, second_ref, third_ref, col_ref, out_ref):
    edge = jnp.where(lax.axis_index("gz") == 0, NK - 1, 0)
    wide = lax.broadcasted_iota(jnp.int32, (NI, NK), 1)
    deep = lax.broadcasted_iota(jnp.int32, (NI, NK), 0)
    out_ref[0:NJ, :] = col_ref[...]
    out_ref[NJ : NJ + 8, :] = jnp.zeros((8, NK), F32)
    for n, beyond in enumerate(beside((first_ref, second_ref, third_ref), slice(0, NI))):
        value = jnp.sum(jnp.where(wide == edge, beyond, 0.0), axis=1, keepdims=True)
        value = jnp.where(wide == deep, jnp.broadcast_to(value, (NI, NK)), 0.0)
        out_ref[NJ + n : NJ + n + 1, :] = jnp.sum(value, axis=0, keepdims=True)


def source_kernel(u_ref, k_ref, sum_ref, skew_ref, first_ref, second_ref, third_ref, f_ref):
    lane = lax.broadcasted_iota(jnp.int32, (8, NK), 1)
    first_lane, last_lane = lane == 0, lane == NK - 1

    def slope(u):
        ahead = jnp.where(last_lane, 0.0, pltpu.roll(u, NK - 1, 1))
        back = jnp.where(first_lane, 0.0, pltpu.roll(u, 1, 1))
        return ahead, ahead - back

    def some(n, nothing):
        base = n * (8 * PITCH)
        near = pl.ds(pl.multiple_of(n * 8, 8), 8)
        deep = pl.ds(pl.multiple_of(NI + n * 8, 8), 8)
        u_below, u_above = beside((first_ref, second_ref, third_ref), near)
        k_below, k_above = beside((first_ref, second_ref, third_ref), deep)

        def tile(ref, j):
            return ref[pl.ds(base + j, 8, stride=PITCH), :]

        u, k = tile(u_ref, 0), tile(k_ref, 0)
        _, d_before = slope(u_below)
        flux_before = (k + k_below) * (u - u_below)
        ahead, d = slope(u)
        for j in range(NJ):
            if j < NJ - 1:
                u_next, k_next = tile(u_ref, j + 1), tile(k_ref, j + 1)
            else:
                u_next, k_next = u_above, k_above
            ahead_next, d_next = slope(u_next)
            flux = (k + k_next) * (u_next - u)
            across = tile(sum_ref, j) * (ahead - u)
            before = jnp.where(first_lane, k * u, pltpu.roll(across, 1, 1))
            f_ref[pl.ds(base + j, 8, stride=PITCH), :] = (
                u
                + (0.5 * ratio_y) * (flux - flux_before)
                + (0.5 * ratio_z) * (across - before)
                + (ratio_mix * tile(skew_ref, j)) * (d_next - d_before)
            )
            u, k, ahead, flux_before, d_before, d = u_next, k_next, ahead_next, flux, d, d_next
        return nothing

    lax.fori_loop(0, NI // 8, some, 0)


def sweep_kernel(
    f0_ref, col_ref, skew_ref, got_ref, t_ref, q_ref, r_ref, plane_ref,
    f_out, b_ref, send_ref, f_ref, sems,
):
    right = lax.axis_index("gz") == 0
    lane, row = lanes(), rows()
    own, far = col_ref[...], got_ref[0:NJ, :]
    own_k, far_k = pltpu.roll(own, NI, 1), pltpu.roll(far, NI, 1)
    below = jnp.broadcast_to(got_ref[NJ : NJ + 1, :], (NJ, NK))
    above = jnp.broadcast_to(got_ref[NJ + 1 : NJ + 2, :], (NJ, NK))
    up = jnp.where(row == NJ - 1, above, pltpu.roll(far, NJ - 1, 0))
    down = jnp.where(row == 0, below, pltpu.roll(far, 1, 0))
    sign = jnp.where(right, ratio_mix, -ratio_mix).astype(F32)
    fluxes = (0.5 * ratio_z) * (own_k * far + far_k * (far - own))
    slopes = sign * (up - down)
    edge = lane == jnp.where(right, NK - 1, 0)
    turn = jnp.where(right, NK - 1, NK)

    def layer(i, state):
        s, total = state
        at = pl.ds(pl.multiple_of(i * NJ, NJ), NJ)
        wide = pl.ds(pl.multiple_of(i * PITCH, 8), NJ)
        shift = (turn - i) & (NK - 1)
        extra = pltpu.roll(fluxes, shift, 1) + skew_ref[wide, :] * pltpu.roll(slopes, shift, 1)
        f = f0_ref[wide, :] + jnp.where(edge, extra, 0.0)
        f_ref[at, :] = f
        s = f + s
        b_ref[at, :] = r_ref[at, :] * s
        total = total + q_ref[at, :] * s
        return t_ref[at, :] * s, total, s

    def leave(n):
        at = pl.ds(pl.multiple_of(n * PART, PART), PART)
        return pltpu.make_async_copy(f_ref.at[at, :], f_out.at[at, :], sems.at[n])

    def some(n, state):
        carried, total, s = state
        for m in range(PART // NJ):
            carried, total, s = layer(n * (PART // NJ) + m, (carried, total))
        leave(n).start()
        return carried, total, s

    zero = jnp.zeros((NJ, NK), F32)
    state = (zero, zero, zero)
    for n in range(ROWS // PART):
        state = some(n, state)
    _, total, s = state
    planes = [plane_ref[c * NJ : c * NJ + NJ, :] for c in range(5)] + [total, s]
    for c, plane in enumerate(planes):
        for q in range(BLOCKS):
            send_ref[q, :, c * NK : c * NK + NK] = plane[2 * q : 2 * q + 2]
    for n in range(ROWS // PART):
        leave(n).wait()


def separator_kernel(got_ref, out_ref):
    half = 0.5 * ratio_x

    def plane(p, c):
        return got_ref[p, :, c * NK : c * NK + NK]

    def inner(p):
        return plane(p, 1)

    def link(p):
        return half * (plane(p, 4) + plane(p + 1, 3))

    middle = BLOCKS // 2
    left, right = [], []
    ground = plane(0, 0) + half * plane(0, 3)
    side = plane(0, 5)
    ground_r = plane(BLOCKS - 1, 2) + half * plane(BLOCKS - 1, 4)
    side_r = plane(BLOCKS - 1, 6)
    for m in range(middle):
        p, o = m, BLOCKS - 1 - m
        r = 1.0 / (ground + inner(p))
        t = inner(p) * r
        left.append((side * r, t))
        ground, side = plane(p, 2) + t * ground, plane(p, 6) + t * side
        r = 1.0 / (ground_r + inner(o))
        t = inner(o) * r
        right.append((side_r * r, t))
        ground_r, side_r = plane(o, 0) + t * ground_r, plane(o, 5) + t * side_r
        if m < middle - 1:
            r = 1.0 / (ground + link(p))
            t = link(p) * r
            left.append((side * r, t))
            ground, side = plane(p + 1, 0) + t * ground, plane(p + 1, 5) + t * side
            r = 1.0 / (ground_r + link(o - 1))
            t = link(o - 1) * r
            right.append((side_r * r, t))
            ground_r, side_r = plane(o - 1, 2) + t * ground_r, plane(o - 1, 6) + t * side_r
    joint = link(middle - 1)
    r = 1.0 / (ground + joint)
    t = joint * r
    left.append((side * r, t))
    value = (side_r + t * side) / (ground_r + t * ground)
    there = value
    values_r = [there]
    for b, t in reversed(right):
        there = b + t * there
        values_r.append(there)
    here = value
    values_l = []
    for b, t in reversed(left):
        here = b + t * here
        values_l.append(here)
    values = values_l[::-1] + values_r
    for n, v in enumerate(values):
        out_ref[2 * n : 2 * n + 2, :] = v


def back_kernel(v_ref, b_ref, t_ref, q_ref, w_out, w_ref, sems):
    half = NJ // 2
    for c in range(4):
        w_ref[pl.ds(c // 2 * NJ + c % 2, half, stride=2), :] = v_ref[pl.ds(c, half, stride=4), :]
    head, tail = w_ref[0:NJ, :], w_ref[NJ : 2 * NJ, :]

    def layer(i, w):
        at = pl.ds(i * NJ, NJ)
        w = (b_ref[at, :] + q_ref[at, :] * head) + t_ref[at, :] * w
        w_ref[at, :] = w
        return w

    w_ref[ROWS - NJ : ROWS, :] = tail
    w = tail
    copies = []
    for n in reversed(range(ROWS // PART)):
        for i in reversed(range(n * (PART // NJ), min((n + 1) * (PART // NJ), NI - 1))):
            w = layer(i, w)
        at = pl.ds(n * PART, PART)
        copies.append(pltpu.make_async_copy(w_ref.at[at, :], w_out.at[at, :], sems.at[n]))
        copies[-1].start()
    for copy in copies:
        copy.wait()


def body(initial_thermal_state, thermal_spread_rate, yz_skew_factor):
    u = initial_thermal_state.reshape(ROWS, NK)
    k = thermal_spread_rate.reshape(ROWS, NK)
    block = ROWS * NK
    single = (NI, NJ, 1, NK)
    anywhere = pl.BlockSpec(memory_space=pltpu.HBM)
    whole = pl.BlockSpec(memory_space=pltpu.VMEM)
    sent = pl.pallas_call(
        edge_kernel,
        out_shape=[pltpu.VMEM((2 * NI, NK), F32)] * 3,
        in_specs=[anywhere] * 2,
        out_specs=[whole] * 3,
        scratch_shapes=[pltpu.SemaphoreType.DMA((6,))],
        compiler_params=pltpu.CompilerParams(vmem_limit_bytes=56 * 1024 * 1024),
        cost_estimate=pl.CostEstimate(flops=0, bytes_accessed=8 * NI * NK * 4, transcendentals=0),
        name="edges",
    )(initial_thermal_state.reshape(single), thermal_spread_rate.reshape(single))
    count = lax.axis_size("gy")
    run = count // 2
    swaps = (
        [(i, i + 1) for i in (*range(1, run - 1, 2), *range(run, count, 2))],
        [(i, i + 1) for i in (*range(0, run - 2, 2), *range(run - 1, count - 1, 2))],
        [(run - 2, run - 1)],
    )
    beyond = [
        lax.ppermute(rows, "gy", [way for a, b in pairs for way in ((a, b), (b, a))])
        for rows, pairs in zip(sent, swaps)
    ]
    spread = (NI * PITCH, NK)
    col, u_wide, k_wide, k_sum = call(
        pack_kernel, [(NJ, NK)] + [spread] * 3, 2, 6 * block, 20 * block, "pack"
    )(u, k)
    t, q, r, planes, skew = call(
        factor_kernel, [(ROWS, NK)] * 3 + [(5 * NJ, NK), spread], 2, 20 * block, 22 * block, "factor"
    )(k, yz_skew_factor)
    (to_half,) = call(corner_kernel, [(NJ + 8, NK)], 4, NI * NK, 0, "corner")(*beyond, col)
    got_col = lax.ppermute(to_half, "gz", [(0, 1), (1, 0)])
    (f0,) = call(source_kernel, [spread], 7, 40 * block, 16 * block, "source")(
        u_wide, k_wide, k_sum, skew, *beyond
    )
    f, b, send = call(
        sweep_kernel, [(ROWS, NK)] * 2 + [(BLOCKS, 2, PLANES * NK)], 8,
        8 * block, 24 * block, "sweep", True,
    )(f0, col, skew, got_col, t, q, r, planes)
    got = lax.all_to_all(send, "gx", 0, 0, tiled=True)
    (values,) = call(
        separator_kernel, [(4 * BLOCKS, NK)], 1, block, block, "separator"
    )(got)
    mine = lax.all_to_all(values, "gx", 0, 0, tiled=True)
    (w,) = call(back_kernel, [(ROWS, NK)], 4, 4 * block, 16 * block, "back", True)(mine, b, t, q)
    shape = initial_thermal_state.shape
    return f.reshape(shape), w.reshape(shape)


def solution(mesh):
    spec = P("gx", "gy", "gz")
    return jax.shard_map(
        body, mesh=mesh, in_specs=(spec, spec, spec), out_specs=(spec, spec), check_vma=False
    )
```

```python
import jax
import jax.numpy as jnp
from jax import lax
from jax.experimental import pallas as pl
from jax.experimental.pallas import tpu as pltpu
from jax.sharding import PartitionSpec as P

ratio_x = 4096.0
ratio_y = 0.2
ratio_z = 0.2
ratio_mix = 0.25

NI, NJ, NK = 64, 32, 128
ROWS = NI * NJ
BLOCKS = 16
PLANES = 7
PART = 512
PITCH = NJ + 8
LONG = 31
F32 = jnp.float32


def call(kernel, outs, n_in, flops, moved, name, leaving=False):
    spec = pl.BlockSpec(memory_space=pltpu.VMEM)
    out_specs = [spec] * len(outs)
    scratch = []
    if leaving:
        out_specs[0] = pl.BlockSpec(memory_space=pl.ANY)
        scratch = [pltpu.VMEM(outs[0], F32), pltpu.SemaphoreType.DMA((ROWS // PART,))]
    return pl.pallas_call(
        kernel,
        out_shape=[jax.ShapeDtypeStruct(shape, F32) for shape in outs],
        in_specs=[spec] * n_in,
        out_specs=out_specs,
        scratch_shapes=scratch,
        compiler_params=pltpu.CompilerParams(vmem_limit_bytes=24 * 1024 * 1024),
        cost_estimate=pl.CostEstimate(flops=flops, bytes_accessed=moved, transcendentals=0),
        name=name,
    )


def lanes():
    return lax.broadcasted_iota(jnp.int32, (NJ, NK), 1)


def rows():
    return lax.broadcasted_iota(jnp.int32, (NJ, NK), 0)


def rows_to_send():
    run = lax.axis_size("gy") // 2
    place = lax.axis_index("gy")
    odd = lax.rem(place, 2) == 1
    lower = place < run
    last = place == run - 1
    ahead = (odd == lower, jnp.where(lower, jnp.logical_or(~odd, last), odd), ~odd)
    return [jnp.where(way, NJ - 1, 0) for way in ahead]


def edge_kernel(u_ref, k_ref, *refs):
    sems = refs[-1]
    copies = []
    for n, (ref, row) in enumerate(zip(refs, rows_to_send())):
        for m, source in enumerate((u_ref, k_ref)):
            copies.append(
                pltpu.make_async_copy(
                    source.at[:, row, 0, :], ref.at[m * NI : m * NI + NI, :], sems.at[2 * n + m]
                )
            )
    for copy in copies:
        copy.start()
    for copy in copies:
        copy.wait()


def by_eights(layer, start):
    def some(n, state):
        for m in range(8):
            state = layer(n * 8 + m, state)
        return state

    return lax.fori_loop(0, NI // 8, some, start)


def pack_kernel(u_ref, k_ref, col_ref, u_wide_ref, k_wide_ref, sum_ref):
    turn = 1 - lax.axis_index("gz")
    lane = lanes()

    def layer(i, col):
        at = pl.ds(pl.multiple_of(i * NJ, NJ), NJ)
        to = pl.ds(pl.multiple_of(i * PITCH, 8), NJ)
        u, k = u_ref[at, :], k_ref[at, :]
        u_wide_ref[to, :] = u
        k_wide_ref[to, :] = k
        sum_ref[to, :] = k + jnp.where(lane == NK - 1, 0.0, pltpu.roll(k, NK - 1, 1))
        col = jnp.where(lane == i, pltpu.roll(u, i + turn, 1), col)
        return jnp.where(lane == i + NI, pltpu.roll(k, (i + (NI + turn)) & (NK - 1), 1), col)

    col_ref[...] = by_eights(layer, jnp.zeros((NJ, NK), F32))


def factor_kernel(k_ref, skew_ref, t_ref, q_ref, r_ref, plane_ref, wide_ref, skew_col_ref):
    turn = 1 - lax.axis_index("gz")
    lane = lanes()

    def widen(i, col):
        g = skew_ref[i].astype(F32)
        wide_ref[pl.ds(pl.multiple_of(i * PITCH, 8), NJ), :] = g
        return jnp.where(lane == i, pltpu.roll(g, i + turn, 1), col)

    half = 0.5 * ratio_x
    zero = jnp.zeros((NJ, NK), F32)
    one = jnp.ones((NJ, NK), F32)
    first = k_ref[0:NJ, :]
    last = k_ref[ROWS - NJ : ROWS, :]
    t_ref[0:NJ, :] = zero
    q_ref[0:NJ, :] = one
    r_ref[0:NJ, :] = zero
    t_ref[ROWS - NJ : ROWS, :] = zero
    q_ref[ROWS - NJ : ROWS, :] = zero
    r_ref[ROWS - NJ : ROWS, :] = zero

    def layer(i, state):
        here, ground, left, total, col = state
        at = pl.ds(pl.multiple_of(i * NJ, NJ), NJ)
        after = k_ref[pl.ds(pl.multiple_of(i * NJ + NJ, NJ), NJ), :]
        link = half * (here + after)
        r = 1.0 / ((ground + left) + link)
        t = link * r
        q = left * r
        t_ref[at, :] = t
        q_ref[at, :] = q
        r_ref[at, :] = r
        return after, 1.0 + t * ground, t * left, total + q * ground, widen(i, col)

    def some(n, state):
        for m in range(LONG):
            state = layer(1 + n * LONG + m, state)
        return state

    second = k_ref[NJ : 2 * NJ, :]
    start = (second, one, half * (first + second), one, widen(0, zero))
    _, ground, left, total, col = lax.fori_loop(0, (NI - 2) // LONG, some, start)
    skew_col_ref[...] = widen(NI - 1, col)
    for c, plane in enumerate((total, left, ground, first, last)):
        plane_ref[c * NJ : c * NJ + NJ, :] = plane


def beside(refs, at):
    run = lax.axis_size("gy") // 2
    place = lax.axis_index("gy")
    odd = lax.rem(place, 2) == 1
    lower = place < run
    last, before = place == run - 1, place == run - 2
    first, second, third = [ref[at, :] for ref in refs]
    below = jnp.where(odd == lower, second, first)
    below = jnp.where(last, third, below)
    above = jnp.where(odd == lower, first, second)
    above = jnp.where(last, second, jnp.where(before, third, above))
    return below, above


def corner_kernel(first_ref, second_ref, third_ref, col_ref, out_ref):
    edge = jnp.where(lax.axis_index("gz") == 0, NK - 1, 0)
    wide = lax.broadcasted_iota(jnp.int32, (NI, NK), 1)
    deep = lax.broadcasted_iota(jnp.int32, (NI, NK), 0)
    out_ref[0:NJ, :] = col_ref[...]
    out_ref[NJ : NJ + 8, :] = jnp.zeros((8, NK), F32)
    for n, beyond in enumerate(beside((first_ref, second_ref, third_ref), slice(0, NI))):
        value = jnp.sum(jnp.where(wide == edge, beyond, 0.0), axis=1, keepdims=True)
        value = jnp.where(wide == deep, jnp.broadcast_to(value, (NI, NK)), 0.0)
        out_ref[NJ + n : NJ + n + 1, :] = jnp.sum(value, axis=0, keepdims=True)


def source_kernel(u_ref, k_ref, sum_ref, skew_ref, first_ref, second_ref, third_ref, f_ref):
    lane = lax.broadcasted_iota(jnp.int32, (8, NK), 1)
    first_lane, last_lane = lane == 0, lane == NK - 1

    def slope(u):
        ahead = jnp.where(last_lane, 0.0, pltpu.roll(u, NK - 1, 1))
        back = jnp.where(first_lane, 0.0, pltpu.roll(u, 1, 1))
        return ahead, ahead - back

    def some(n, nothing):
        base = n * (8 * PITCH)
        near = pl.ds(pl.multiple_of(n * 8, 8), 8)
        deep = pl.ds(pl.multiple_of(NI + n * 8, 8), 8)
        u_below, u_above = beside((first_ref, second_ref, third_ref), near)
        k_below, k_above = beside((first_ref, second_ref, third_ref), deep)

        def tile(ref, j):
            return ref[pl.ds(base + j, 8, stride=PITCH), :]

        u, k = tile(u_ref, 0), tile(k_ref, 0)
        _, d_before = slope(u_below)
        flux_before = (k + k_below) * (u - u_below)
        ahead, d = slope(u)
        for j in range(NJ):
            if j < NJ - 1:
                u_next, k_next = tile(u_ref, j + 1), tile(k_ref, j + 1)
            else:
                u_next, k_next = u_above, k_above
            ahead_next, d_next = slope(u_next)
            flux = (k + k_next) * (u_next - u)
            across = tile(sum_ref, j) * (ahead - u)
            before = jnp.where(first_lane, k * u, pltpu.roll(across, 1, 1))
            f_ref[pl.ds(base + j, 8, stride=PITCH), :] = (
                u
                + (0.5 * ratio_y) * (flux - flux_before)
                + (0.5 * ratio_z) * (across - before)
                + (ratio_mix * tile(skew_ref, j)) * (d_next - d_before)
            )
            u, k, ahead, flux_before, d_before, d = u_next, k_next, ahead_next, flux, d, d_next
        return nothing

    lax.fori_loop(0, NI // 8, some, 0)


def sweep_kernel(
    f0_ref, col_ref, skew_col_ref, got_ref, t_ref, q_ref, r_ref, plane_ref,
    f_out, b_ref, send_ref, f_ref, sems,
):
    right = lax.axis_index("gz") == 0
    lane, row = lanes(), rows()
    own, far = col_ref[...], got_ref[0:NJ, :]
    own_k, far_k = pltpu.roll(own, NI, 1), pltpu.roll(far, NI, 1)
    below = jnp.broadcast_to(got_ref[NJ : NJ + 1, :], (NJ, NK))
    above = jnp.broadcast_to(got_ref[NJ + 1 : NJ + 2, :], (NJ, NK))
    up = jnp.where(row == NJ - 1, above, pltpu.roll(far, NJ - 1, 0))
    down = jnp.where(row == 0, below, pltpu.roll(far, 1, 0))
    sign = jnp.where(right, ratio_mix, -ratio_mix).astype(F32)
    extra = (0.5 * ratio_z) * (own_k * far + far_k * (far - own)) + (
        sign * skew_col_ref[...]
    ) * (up - down)
    edge = lane == jnp.where(right, NK - 1, 0)
    turn = jnp.where(right, NK - 1, NK)

    def layer(i, state):
        s, total = state
        at = pl.ds(pl.multiple_of(i * NJ, NJ), NJ)
        here = pltpu.roll(extra, (turn - i) & (NK - 1), 1)
        f = f0_ref[pl.ds(pl.multiple_of(i * PITCH, 8), NJ), :] + jnp.where(edge, here, 0.0)
        f_ref[at, :] = f
        s = f + s
        b_ref[at, :] = r_ref[at, :] * s
        total = total + q_ref[at, :] * s
        return t_ref[at, :] * s, total, s

    def leave(n):
        at = pl.ds(pl.multiple_of(n * PART, PART), PART)
        return pltpu.make_async_copy(f_ref.at[at, :], f_out.at[at, :], sems.at[n])

    def some(n, state):
        carried, total, s = state
        for m in range(PART // NJ):
            carried, total, s = layer(n * (PART // NJ) + m, (carried, total))
        leave(n).start()
        return carried, total, s

    zero = jnp.zeros((NJ, NK), F32)
    state = (zero, zero, zero)
    for n in range(ROWS // PART):
        state = some(n, state)
    _, total, s = state
    planes = [plane_ref[c * NJ : c * NJ + NJ, :] for c in range(5)] + [total, s]
    for c, plane in enumerate(planes):
        for q in range(BLOCKS):
            send_ref[q, :, c * NK : c * NK + NK] = plane[2 * q : 2 * q + 2]
    for n in range(ROWS // PART):
        leave(n).wait()


def separator_kernel(got_ref, out_ref):
    half = 0.5 * ratio_x

    def plane(p, c):
        return got_ref[p, :, c * NK : c * NK + NK]

    def inner(p):
        return plane(p, 1)

    def link(p):
        return half * (plane(p, 4) + plane(p + 1, 3))

    middle = BLOCKS // 2
    left, right = [], []
    ground = plane(0, 0) + half * plane(0, 3)
    side = plane(0, 5)
    ground_r = plane(BLOCKS - 1, 2) + half * plane(BLOCKS - 1, 4)
    side_r = plane(BLOCKS - 1, 6)
    for m in range(middle):
        p, o = m, BLOCKS - 1 - m
        r = 1.0 / (ground + inner(p))
        t = inner(p) * r
        left.append((side * r, t))
        ground, side = plane(p, 2) + t * ground, plane(p, 6) + t * side
        r = 1.0 / (ground_r + inner(o))
        t = inner(o) * r
        right.append((side_r * r, t))
        ground_r, side_r = plane(o, 0) + t * ground_r, plane(o, 5) + t * side_r
        if m < middle - 1:
            r = 1.0 / (ground + link(p))
            t = link(p) * r
            left.append((side * r, t))
            ground, side = plane(p + 1, 0) + t * ground, plane(p + 1, 5) + t * side
            r = 1.0 / (ground_r + link(o - 1))
            t = link(o - 1) * r
            right.append((side_r * r, t))
            ground_r, side_r = plane(o - 1, 2) + t * ground_r, plane(o - 1, 6) + t * side_r
    joint = link(middle - 1)
    r = 1.0 / (ground + joint)
    t = joint * r
    left.append((side * r, t))
    value = (side_r + t * side) / (ground_r + t * ground)
    there = value
    values_r = [there]
    for b, t in reversed(right):
        there = b + t * there
        values_r.append(there)
    here = value
    values_l = []
    for b, t in reversed(left):
        here = b + t * here
        values_l.append(here)
    values = values_l[::-1] + values_r
    for n, v in enumerate(values):
        out_ref[2 * n : 2 * n + 2, :] = v


def back_kernel(v_ref, b_ref, t_ref, q_ref, w_out, w_ref, sems):
    half = NJ // 2
    for c in range(4):
        w_ref[pl.ds(c // 2 * NJ + c % 2, half, stride=2), :] = v_ref[pl.ds(c, half, stride=4), :]
    head, tail = w_ref[0:NJ, :], w_ref[NJ : 2 * NJ, :]

    def layer(i, w):
        at = pl.ds(i * NJ, NJ)
        w = (b_ref[at, :] + q_ref[at, :] * head) + t_ref[at, :] * w
        w_ref[at, :] = w
        return w

    w_ref[ROWS - NJ : ROWS, :] = tail
    w = tail
    copies = []
    for n in reversed(range(ROWS // PART)):
        for i in reversed(range(n * (PART // NJ), min((n + 1) * (PART // NJ), NI - 1))):
            w = layer(i, w)
        at = pl.ds(n * PART, PART)
        copies.append(pltpu.make_async_copy(w_ref.at[at, :], w_out.at[at, :], sems.at[n]))
        copies[-1].start()
    for copy in copies:
        copy.wait()


def body(initial_thermal_state, thermal_spread_rate, yz_skew_factor):
    u = initial_thermal_state.reshape(ROWS, NK)
    k = thermal_spread_rate.reshape(ROWS, NK)
    block = ROWS * NK
    single = (NI, NJ, 1, NK)
    anywhere = pl.BlockSpec(memory_space=pltpu.HBM)
    whole = pl.BlockSpec(memory_space=pltpu.VMEM)
    sent = pl.pallas_call(
        edge_kernel,
        out_shape=[pltpu.VMEM((2 * NI, NK), F32)] * 3,
        in_specs=[anywhere] * 2,
        out_specs=[whole] * 3,
        scratch_shapes=[pltpu.SemaphoreType.DMA((6,))],
        compiler_params=pltpu.CompilerParams(vmem_limit_bytes=56 * 1024 * 1024),
        cost_estimate=pl.CostEstimate(flops=0, bytes_accessed=8 * NI * NK * 4, transcendentals=0),
        name="edges",
    )(initial_thermal_state.reshape(single), thermal_spread_rate.reshape(single))
    count = lax.axis_size("gy")
    run = count // 2
    swaps = (
        [(i, i + 1) for i in (*range(1, run - 1, 2), *range(run, count, 2))],
        [(i, i + 1) for i in (*range(0, run - 2, 2), *range(run - 1, count - 1, 2))],
        [(run - 2, run - 1)],
    )
    beyond = [
        lax.ppermute(rows, "gy", [way for a, b in pairs for way in ((a, b), (b, a))])
        for rows, pairs in zip(sent, swaps)
    ]
    spread = (NI * PITCH, NK)
    col, u_wide, k_wide, k_sum = call(
        pack_kernel, [(NJ, NK)] + [spread] * 3, 2, 6 * block, 20 * block, "pack"
    )(u, k)
    t, q, r, planes, skew, skew_col = call(
        factor_kernel, [(ROWS, NK)] * 3 + [(5 * NJ, NK), spread, (NJ, NK)], 2, 20 * block, 22 * block, "factor"
    )(k, yz_skew_factor)
    (to_half,) = call(corner_kernel, [(NJ + 8, NK)], 4, NI * NK, 0, "corner")(*beyond, col)
    got_col = lax.ppermute(to_half, "gz", [(0, 1), (1, 0)])
    (f0,) = call(source_kernel, [spread], 7, 40 * block, 16 * block, "source")(
        u_wide, k_wide, k_sum, skew, *beyond
    )
    f, b, send = call(
        sweep_kernel, [(ROWS, NK)] * 2 + [(BLOCKS, 2, PLANES * NK)], 8,
        8 * block, 24 * block, "sweep", True,
    )(f0, col, skew_col, got_col, t, q, r, planes)
    got = lax.all_to_all(send, "gx", 0, 0, tiled=True)
    (values,) = call(
        separator_kernel, [(4 * BLOCKS, NK)], 1, block, block, "separator"
    )(got)
    mine = lax.all_to_all(values, "gx", 0, 0, tiled=True)
    (w,) = call(back_kernel, [(ROWS, NK)], 4, 4 * block, 16 * block, "back", True)(mine, b, t, q)
    shape = initial_thermal_state.shape
    return f.reshape(shape), w.reshape(shape)


def solution(mesh):
    spec = P("gx", "gy", "gz")
    return jax.shard_map(
        body, mesh=mesh, in_specs=(spec, spec, spec), out_specs=(spec, spec), check_vma=False
    )
```

```python
import jax
import jax.numpy as jnp
from jax import lax
from jax.experimental import pallas as pl
from jax.experimental.pallas import tpu as pltpu
from jax.sharding import PartitionSpec as P

ratio_x = 4096.0
ratio_y = 0.2
ratio_z = 0.2
ratio_mix = 0.25

NI, NJ, NK = 64, 32, 128
ROWS = NI * NJ
BLOCKS = 16
PLANES = 7
PART = 512
PITCH = NJ + 8
LONG = 31
F32 = jnp.float32


def call(kernel, outs, n_in, flops, moved, name, leaving=False):
    spec = pl.BlockSpec(memory_space=pltpu.VMEM)
    out_specs = [spec] * len(outs)
    scratch = []
    if leaving:
        out_specs[0] = pl.BlockSpec(memory_space=pl.ANY)
        scratch = [pltpu.VMEM(outs[0], F32), pltpu.SemaphoreType.DMA((ROWS // PART,))]
    return pl.pallas_call(
        kernel,
        out_shape=[jax.ShapeDtypeStruct(shape, F32) for shape in outs],
        in_specs=[spec] * n_in,
        out_specs=out_specs,
        scratch_shapes=scratch,
        compiler_params=pltpu.CompilerParams(vmem_limit_bytes=24 * 1024 * 1024),
        cost_estimate=pl.CostEstimate(flops=flops, bytes_accessed=moved, transcendentals=0),
        name=name,
    )


def lanes():
    return lax.broadcasted_iota(jnp.int32, (NJ, NK), 1)


def rows():
    return lax.broadcasted_iota(jnp.int32, (NJ, NK), 0)


def rows_to_send():
    run = lax.axis_size("gy") // 2
    place = lax.axis_index("gy")
    odd = lax.rem(place, 2) == 1
    lower = place < run
    last = place == run - 1
    ahead = (odd == lower, jnp.where(lower, jnp.logical_or(~odd, last), odd), ~odd)
    return [jnp.where(way, NJ - 1, 0) for way in ahead]


def edge_kernel(u_ref, k_ref, *refs):
    sems = refs[-1]
    copies = []
    for n, (ref, row) in enumerate(zip(refs, rows_to_send())):
        for m, source in enumerate((u_ref, k_ref)):
            copies.append(
                pltpu.make_async_copy(
                    source.at[:, row, 0, :], ref.at[m * NI : m * NI + NI, :], sems.at[2 * n + m]
                )
            )
    for copy in copies:
        copy.start()
    for copy in copies:
        copy.wait()


def by_eights(layer, start):
    def some(n, state):
        for m in range(8):
            state = layer(n * 8 + m, state)
        return state

    return lax.fori_loop(0, NI // 8, some, start)


def pack_kernel(u_ref, k_ref, col_ref, u_wide_ref, k_wide_ref):
    turn = 1 - lax.axis_index("gz")
    lane = lanes()

    def layer(i, col):
        at = pl.ds(pl.multiple_of(i * NJ, NJ), NJ)
        to = pl.ds(pl.multiple_of(i * PITCH, 8), NJ)
        u, k = u_ref[at, :], k_ref[at, :]
        u_wide_ref[to, :] = u
        k_wide_ref[to, :] = k
        col = jnp.where(lane == i, pltpu.roll(u, i + turn, 1), col)
        return jnp.where(lane == i + NI, pltpu.roll(k, (i + (NI + turn)) & (NK - 1), 1), col)

    col_ref[...] = by_eights(layer, jnp.zeros((NJ, NK), F32))


def factor_kernel(k_ref, skew_ref, t_ref, q_ref, r_ref, plane_ref, wide_ref, skew_col_ref, sum_ref):
    turn = 1 - lax.axis_index("gz")
    lane = lanes()

    def widen(i, col):
        g = skew_ref[i].astype(F32)
        k = k_ref[pl.ds(pl.multiple_of(i * NJ, NJ), NJ), :]
        to = pl.ds(pl.multiple_of(i * PITCH, 8), NJ)
        wide_ref[to, :] = g
        sum_ref[to, :] = k + jnp.where(lane == NK - 1, 0.0, pltpu.roll(k, NK - 1, 1))
        return jnp.where(lane == i, pltpu.roll(g, i + turn, 1), col)

    half = 0.5 * ratio_x
    zero = jnp.zeros((NJ, NK), F32)
    one = jnp.ones((NJ, NK), F32)
    first = k_ref[0:NJ, :]
    last = k_ref[ROWS - NJ : ROWS, :]
    t_ref[0:NJ, :] = zero
    q_ref[0:NJ, :] = one
    r_ref[0:NJ, :] = zero
    t_ref[ROWS - NJ : ROWS, :] = zero
    q_ref[ROWS - NJ : ROWS, :] = zero
    r_ref[ROWS - NJ : ROWS, :] = zero

    def layer(i, state):
        here, ground, left, total, col = state
        at = pl.ds(pl.multiple_of(i * NJ, NJ), NJ)
        after = k_ref[pl.ds(pl.multiple_of(i * NJ + NJ, NJ), NJ), :]
        link = half * (here + after)
        r = 1.0 / ((ground + left) + link)
        t = link * r
        q = left * r
        t_ref[at, :] = t
        q_ref[at, :] = q
        r_ref[at, :] = r
        return after, 1.0 + t * ground, t * left, total + q * ground, widen(i, col)

    def some(n, state):
        for m in range(LONG):
            state = layer(1 + n * LONG + m, state)
        return state

    second = k_ref[NJ : 2 * NJ, :]
    start = (second, one, half * (first + second), one, widen(0, zero))
    _, ground, left, total, col = lax.fori_loop(0, (NI - 2) // LONG, some, start)
    skew_col_ref[...] = widen(NI - 1, col)
    for c, plane in enumerate((total, left, ground, first, last)):
        plane_ref[c * NJ : c * NJ + NJ, :] = plane


def beside(refs, at):
    run = lax.axis_size("gy") // 2
    place = lax.axis_index("gy")
    odd = lax.rem(place, 2) == 1
    lower = place < run
    last, before = place == run - 1, place == run - 2
    first, second, third = [ref[at, :] for ref in refs]
    below = jnp.where(odd == lower, second, first)
    below = jnp.where(last, third, below)
    above = jnp.where(odd == lower, first, second)
    above = jnp.where(last, second, jnp.where(before, third, above))
    return below, above


def corner_kernel(first_ref, second_ref, third_ref, col_ref, out_ref):
    edge = jnp.where(lax.axis_index("gz") == 0, NK - 1, 0)
    wide = lax.broadcasted_iota(jnp.int32, (NI, NK), 1)
    deep = lax.broadcasted_iota(jnp.int32, (NI, NK), 0)
    out_ref[0:NJ, :] = col_ref[...]
    out_ref[NJ : NJ + 8, :] = jnp.zeros((8, NK), F32)
    for n, beyond in enumerate(beside((first_ref, second_ref, third_ref), slice(0, NI))):
        value = jnp.sum(jnp.where(wide == edge, beyond, 0.0), axis=1, keepdims=True)
        value = jnp.where(wide == deep, jnp.broadcast_to(value, (NI, NK)), 0.0)
        out_ref[NJ + n : NJ + n + 1, :] = jnp.sum(value, axis=0, keepdims=True)


def source_kernel(u_ref, k_ref, sum_ref, skew_ref, first_ref, second_ref, third_ref, f_ref):
    lane = lax.broadcasted_iota(jnp.int32, (8, NK), 1)
    first_lane, last_lane = lane == 0, lane == NK - 1

    def slope(u):
        ahead = jnp.where(last_lane, 0.0, pltpu.roll(u, NK - 1, 1))
        back = jnp.where(first_lane, 0.0, pltpu.roll(u, 1, 1))
        return ahead, ahead - back

    def some(n, nothing):
        base = n * (8 * PITCH)
        near = pl.ds(pl.multiple_of(n * 8, 8), 8)
        deep = pl.ds(pl.multiple_of(NI + n * 8, 8), 8)
        u_below, u_above = beside((first_ref, second_ref, third_ref), near)
        k_below, k_above = beside((first_ref, second_ref, third_ref), deep)

        def tile(ref, j):
            return ref[pl.ds(base + j, 8, stride=PITCH), :]

        u, k = tile(u_ref, 0), tile(k_ref, 0)
        _, d_before = slope(u_below)
        flux_before = (k + k_below) * (u - u_below)
        ahead, d = slope(u)
        for j in range(NJ):
            if j < NJ - 1:
                u_next, k_next = tile(u_ref, j + 1), tile(k_ref, j + 1)
            else:
                u_next, k_next = u_above, k_above
            ahead_next, d_next = slope(u_next)
            flux = (k + k_next) * (u_next - u)
            across = tile(sum_ref, j) * (ahead - u)
            before = jnp.where(first_lane, k * u, pltpu.roll(across, 1, 1))
            f_ref[pl.ds(base + j, 8, stride=PITCH), :] = (
                u
                + (0.5 * ratio_y) * (flux - flux_before)
                + (0.5 * ratio_z) * (across - before)
                + (ratio_mix * tile(skew_ref, j)) * (d_next - d_before)
            )
            u, k, ahead, flux_before, d_before, d = u_next, k_next, ahead_next, flux, d, d_next
        return nothing

    lax.fori_loop(0, NI // 8, some, 0)


def sweep_kernel(
    f0_ref, col_ref, skew_col_ref, got_ref, t_ref, q_ref, r_ref, plane_ref,
    f_out, b_ref, send_ref, f_ref, sems,
):
    right = lax.axis_index("gz") == 0
    lane, row = lanes(), rows()
    own, far = col_ref[...], got_ref[0:NJ, :]
    own_k, far_k = pltpu.roll(own, NI, 1), pltpu.roll(far, NI, 1)
    below = jnp.broadcast_to(got_ref[NJ : NJ + 1, :], (NJ, NK))
    above = jnp.broadcast_to(got_ref[NJ + 1 : NJ + 2, :], (NJ, NK))
    up = jnp.where(row == NJ - 1, above, pltpu.roll(far, NJ - 1, 0))
    down = jnp.where(row == 0, below, pltpu.roll(far, 1, 0))
    sign = jnp.where(right, ratio_mix, -ratio_mix).astype(F32)
    extra = (0.5 * ratio_z) * (own_k * far + far_k * (far - own)) + (
        sign * skew_col_ref[...]
    ) * (up - down)
    edge = lane == jnp.where(right, NK - 1, 0)
    turn = jnp.where(right, NK - 1, NK)

    def layer(i, state):
        s, total = state
        at = pl.ds(pl.multiple_of(i * NJ, NJ), NJ)
        here = pltpu.roll(extra, (turn - i) & (NK - 1), 1)
        f = f0_ref[pl.ds(pl.multiple_of(i * PITCH, 8), NJ), :] + jnp.where(edge, here, 0.0)
        f_ref[at, :] = f
        s = f + s
        b_ref[at, :] = r_ref[at, :] * s
        total = total + q_ref[at, :] * s
        return t_ref[at, :] * s, total, s

    def leave(n):
        at = pl.ds(pl.multiple_of(n * PART, PART), PART)
        return pltpu.make_async_copy(f_ref.at[at, :], f_out.at[at, :], sems.at[n])

    def some(n, state):
        carried, total, s = state
        for m in range(PART // NJ):
            carried, total, s = layer(n * (PART // NJ) + m, (carried, total))
        leave(n).start()
        return carried, total, s

    zero = jnp.zeros((NJ, NK), F32)
    state = (zero, zero, zero)
    for n in range(ROWS // PART):
        state = some(n, state)
    _, total, s = state
    planes = [plane_ref[c * NJ : c * NJ + NJ, :] for c in range(5)] + [total, s]
    for c, plane in enumerate(planes):
        for q in range(BLOCKS):
            send_ref[q, :, c * NK : c * NK + NK] = plane[2 * q : 2 * q + 2]
    for n in range(ROWS // PART):
        leave(n).wait()


def separator_kernel(got_ref, out_ref):
    half = 0.5 * ratio_x

    def plane(p, c):
        return got_ref[p, :, c * NK : c * NK + NK]

    def inner(p):
        return plane(p, 1)

    def link(p):
        return half * (plane(p, 4) + plane(p + 1, 3))

    middle = BLOCKS // 2
    left, right = [], []
    ground = plane(0, 0) + half * plane(0, 3)
    side = plane(0, 5)
    ground_r = plane(BLOCKS - 1, 2) + half * plane(BLOCKS - 1, 4)
    side_r = plane(BLOCKS - 1, 6)
    for m in range(middle):
        p, o = m, BLOCKS - 1 - m
        r = 1.0 / (ground + inner(p))
        t = inner(p) * r
        left.append((side * r, t))
        ground, side = plane(p, 2) + t * ground, plane(p, 6) + t * side
        r = 1.0 / (ground_r + inner(o))
        t = inner(o) * r
        right.append((side_r * r, t))
        ground_r, side_r = plane(o, 0) + t * ground_r, plane(o, 5) + t * side_r
        if m < middle - 1:
            r = 1.0 / (ground + link(p))
            t = link(p) * r
            left.append((side * r, t))
            ground, side = plane(p + 1, 0) + t * ground, plane(p + 1, 5) + t * side
            r = 1.0 / (ground_r + link(o - 1))
            t = link(o - 1) * r
            right.append((side_r * r, t))
            ground_r, side_r = plane(o - 1, 2) + t * ground_r, plane(o - 1, 6) + t * side_r
    joint = link(middle - 1)
    r = 1.0 / (ground + joint)
    t = joint * r
    left.append((side * r, t))
    value = (side_r + t * side) / (ground_r + t * ground)
    there = value
    values_r = [there]
    for b, t in reversed(right):
        there = b + t * there
        values_r.append(there)
    here = value
    values_l = []
    for b, t in reversed(left):
        here = b + t * here
        values_l.append(here)
    values = values_l[::-1] + values_r
    for n, v in enumerate(values):
        out_ref[2 * n : 2 * n + 2, :] = v


def back_kernel(v_ref, b_ref, t_ref, q_ref, w_out, w_ref, sems):
    half = NJ // 2
    for c in range(4):
        w_ref[pl.ds(c // 2 * NJ + c % 2, half, stride=2), :] = v_ref[pl.ds(c, half, stride=4), :]
    head, tail = w_ref[0:NJ, :], w_ref[NJ : 2 * NJ, :]

    def layer(i, w):
        at = pl.ds(i * NJ, NJ)
        w = (b_ref[at, :] + q_ref[at, :] * head) + t_ref[at, :] * w
        w_ref[at, :] = w
        return w

    w_ref[ROWS - NJ : ROWS, :] = tail
    w = tail
    copies = []
    for n in reversed(range(ROWS // PART)):
        for i in reversed(range(n * (PART // NJ), min((n + 1) * (PART // NJ), NI - 1))):
            w = layer(i, w)
        at = pl.ds(n * PART, PART)
        copies.append(pltpu.make_async_copy(w_ref.at[at, :], w_out.at[at, :], sems.at[n]))
        copies[-1].start()
    for copy in copies:
        copy.wait()


def body(initial_thermal_state, thermal_spread_rate, yz_skew_factor):
    u = initial_thermal_state.reshape(ROWS, NK)
    k = thermal_spread_rate.reshape(ROWS, NK)
    block = ROWS * NK
    single = (NI, NJ, 1, NK)
    anywhere = pl.BlockSpec(memory_space=pltpu.HBM)
    whole = pl.BlockSpec(memory_space=pltpu.VMEM)
    sent = pl.pallas_call(
        edge_kernel,
        out_shape=[pltpu.VMEM((2 * NI, NK), F32)] * 3,
        in_specs=[anywhere] * 2,
        out_specs=[whole] * 3,
        scratch_shapes=[pltpu.SemaphoreType.DMA((6,))],
        compiler_params=pltpu.CompilerParams(vmem_limit_bytes=56 * 1024 * 1024),
        cost_estimate=pl.CostEstimate(flops=0, bytes_accessed=8 * NI * NK * 4, transcendentals=0),
        name="edges",
    )(initial_thermal_state.reshape(single), thermal_spread_rate.reshape(single))
    count = lax.axis_size("gy")
    run = count // 2
    swaps = (
        [(i, i + 1) for i in (*range(1, run - 1, 2), *range(run, count, 2))],
        [(i, i + 1) for i in (*range(0, run - 2, 2), *range(run - 1, count - 1, 2))],
        [(run - 2, run - 1)],
    )
    beyond = [
        lax.ppermute(rows, "gy", [way for a, b in pairs for way in ((a, b), (b, a))])
        for rows, pairs in zip(sent, swaps)
    ]
    spread = (NI * PITCH, NK)
    col, u_wide, k_wide = call(
        pack_kernel, [(NJ, NK)] + [spread] * 2, 2, 6 * block, 20 * block, "pack"
    )(u, k)
    t, q, r, planes, skew, skew_col, k_sum = call(
        factor_kernel, [(ROWS, NK)] * 3 + [(5 * NJ, NK), spread, (NJ, NK), spread], 2, 20 * block, 22 * block, "factor"
    )(k, yz_skew_factor)
    (to_half,) = call(corner_kernel, [(NJ + 8, NK)], 4, NI * NK, 0, "corner")(*beyond, col)
    got_col = lax.ppermute(to_half, "gz", [(0, 1), (1, 0)])
    (f0,) = call(source_kernel, [spread], 7, 40 * block, 16 * block, "source")(
        u_wide, k_wide, k_sum, skew, *beyond
    )
    f, b, send = call(
        sweep_kernel, [(ROWS, NK)] * 2 + [(BLOCKS, 2, PLANES * NK)], 8,
        8 * block, 24 * block, "sweep", True,
    )(f0, col, skew_col, got_col, t, q, r, planes)
    got = lax.all_to_all(send, "gx", 0, 0, tiled=True)
    (values,) = call(
        separator_kernel, [(4 * BLOCKS, NK)], 1, block, block, "separator"
    )(got)
    mine = lax.all_to_all(values, "gx", 0, 0, tiled=True)
    (w,) = call(back_kernel, [(ROWS, NK)], 4, 4 * block, 16 * block, "back", True)(mine, b, t, q)
    shape = initial_thermal_state.shape
    return f.reshape(shape), w.reshape(shape)


def solution(mesh):
    spec = P("gx", "gy", "gz")
    return jax.shard_map(
        body, mesh=mesh, in_specs=(spec, spec, spec), out_specs=(spec, spec), check_vma=False
    )
```

```python
import jax
import jax.numpy as jnp
from jax import lax
from jax.experimental import pallas as pl
from jax.experimental.pallas import tpu as pltpu
from jax.sharding import PartitionSpec as P

ratio_x = 4096.0
ratio_y = 0.2
ratio_z = 0.2
ratio_mix = 0.25

NI, NJ, NK = 64, 32, 128
ROWS = NI * NJ
BLOCKS = 16
PLANES = 7
PART = 512
PITCH = NJ + 8
LONG = 62
F32 = jnp.float32


def call(kernel, outs, n_in, flops, moved, name, leaving=False):
    spec = pl.BlockSpec(memory_space=pltpu.VMEM)
    out_specs = [spec] * len(outs)
    scratch = []
    if leaving:
        out_specs[0] = pl.BlockSpec(memory_space=pl.ANY)
        scratch = [pltpu.VMEM(outs[0], F32), pltpu.SemaphoreType.DMA((ROWS // PART,))]
    return pl.pallas_call(
        kernel,
        out_shape=[jax.ShapeDtypeStruct(shape, F32) for shape in outs],
        in_specs=[spec] * n_in,
        out_specs=out_specs,
        scratch_shapes=scratch,
        compiler_params=pltpu.CompilerParams(vmem_limit_bytes=24 * 1024 * 1024),
        cost_estimate=pl.CostEstimate(flops=flops, bytes_accessed=moved, transcendentals=0),
        name=name,
    )


def lanes():
    return lax.broadcasted_iota(jnp.int32, (NJ, NK), 1)


def rows():
    return lax.broadcasted_iota(jnp.int32, (NJ, NK), 0)


def rows_to_send():
    run = lax.axis_size("gy") // 2
    place = lax.axis_index("gy")
    odd = lax.rem(place, 2) == 1
    lower = place < run
    last = place == run - 1
    ahead = (odd == lower, jnp.where(lower, jnp.logical_or(~odd, last), odd), ~odd)
    return [jnp.where(way, NJ - 1, 0) for way in ahead]


def edge_kernel(u_ref, k_ref, *refs):
    sems = refs[-1]
    copies = []
    for n, (ref, row) in enumerate(zip(refs, rows_to_send())):
        for m, source in enumerate((u_ref, k_ref)):
            copies.append(
                pltpu.make_async_copy(
                    source.at[:, row, 0, :], ref.at[m * NI : m * NI + NI, :], sems.at[2 * n + m]
                )
            )
    for copy in copies:
        copy.start()
    for copy in copies:
        copy.wait()


def by_eights(layer, start):
    def some(n, state):
        for m in range(8):
            state = layer(n * 8 + m, state)
        return state

    return lax.fori_loop(0, NI // 8, some, start)


def pack_kernel(u_ref, k_ref, col_ref, u_wide_ref, k_wide_ref, sum_ref):
    turn = 1 - lax.axis_index("gz")
    lane = lanes()

    def layer(i, col):
        at = pl.ds(pl.multiple_of(i * NJ, NJ), NJ)
        to = pl.ds(pl.multiple_of(i * PITCH, 8), NJ)
        u, k = u_ref[at, :], k_ref[at, :]
        u_wide_ref[to, :] = u
        k_wide_ref[to, :] = k
        sum_ref[to, :] = k + jnp.where(lane == NK - 1, 0.0, pltpu.roll(k, NK - 1, 1))
        col = jnp.where(lane == i, pltpu.roll(u, i + turn, 1), col)
        return jnp.where(lane == i + NI, pltpu.roll(k, (i + (NI + turn)) & (NK - 1), 1), col)

    col_ref[...] = by_eights(layer, jnp.zeros((NJ, NK), F32))


def factor_kernel(k_ref, skew_ref, t_ref, q_ref, r_ref, plane_ref, wide_ref, skew_col_ref):
    turn = 1 - lax.axis_index("gz")
    lane = lanes()

    def widen(i, col):
        g = skew_ref[i].astype(F32)
        wide_ref[pl.ds(pl.multiple_of(i * PITCH, 8), NJ), :] = g
        return jnp.where(lane == i, pltpu.roll(g, i + turn, 1), col)

    half = 0.5 * ratio_x
    zero = jnp.zeros((NJ, NK), F32)
    one = jnp.ones((NJ, NK), F32)
    first = k_ref[0:NJ, :]
    last = k_ref[ROWS - NJ : ROWS, :]
    t_ref[0:NJ, :] = zero
    q_ref[0:NJ, :] = one
    r_ref[0:NJ, :] = zero
    t_ref[ROWS - NJ : ROWS, :] = zero
    q_ref[ROWS - NJ : ROWS, :] = zero
    r_ref[ROWS - NJ : ROWS, :] = zero

    def layer(i, state):
        here, ground, left, total, col = state
        at = pl.ds(pl.multiple_of(i * NJ, NJ), NJ)
        after = k_ref[pl.ds(pl.multiple_of(i * NJ + NJ, NJ), NJ), :]
        link = half * (here + after)
        r = 1.0 / ((ground + left) + link)
        t = link * r
        q = left * r
        t_ref[at, :] = t
        q_ref[at, :] = q
        r_ref[at, :] = r
        return after, 1.0 + t * ground, t * left, total + q * ground, widen(i, col)

    def some(n, state):
        for m in range(LONG):
            state = layer(1 + n * LONG + m, state)
        return state

    second = k_ref[NJ : 2 * NJ, :]
    start = (second, one, half * (first + second), one, widen(0, zero))
    _, ground, left, total, col = lax.fori_loop(0, (NI - 2) // LONG, some, start)
    skew_col_ref[...] = widen(NI - 1, col)
    for c, plane in enumerate((total, left, ground, first, last)):
        plane_ref[c * NJ : c * NJ + NJ, :] = plane


def beside(refs, at):
    run = lax.axis_size("gy") // 2
    place = lax.axis_index("gy")
    odd = lax.rem(place, 2) == 1
    lower = place < run
    last, before = place == run - 1, place == run - 2
    first, second, third = [ref[at, :] for ref in refs]
    below = jnp.where(odd == lower, second, first)
    below = jnp.where(last, third, below)
    above = jnp.where(odd == lower, first, second)
    above = jnp.where(last, second, jnp.where(before, third, above))
    return below, above


def corner_kernel(first_ref, second_ref, third_ref, col_ref, out_ref):
    edge = jnp.where(lax.axis_index("gz") == 0, NK - 1, 0)
    wide = lax.broadcasted_iota(jnp.int32, (NI, NK), 1)
    deep = lax.broadcasted_iota(jnp.int32, (NI, NK), 0)
    out_ref[0:NJ, :] = col_ref[...]
    out_ref[NJ : NJ + 8, :] = jnp.zeros((8, NK), F32)
    for n, beyond in enumerate(beside((first_ref, second_ref, third_ref), slice(0, NI))):
        value = jnp.sum(jnp.where(wide == edge, beyond, 0.0), axis=1, keepdims=True)
        value = jnp.where(wide == deep, jnp.broadcast_to(value, (NI, NK)), 0.0)
        out_ref[NJ + n : NJ + n + 1, :] = jnp.sum(value, axis=0, keepdims=True)


def source_kernel(u_ref, k_ref, sum_ref, skew_ref, first_ref, second_ref, third_ref, f_ref):
    lane = lax.broadcasted_iota(jnp.int32, (8, NK), 1)
    first_lane, last_lane = lane == 0, lane == NK - 1

    def slope(u):
        ahead = jnp.where(last_lane, 0.0, pltpu.roll(u, NK - 1, 1))
        back = jnp.where(first_lane, 0.0, pltpu.roll(u, 1, 1))
        return ahead, ahead - back

    def some(n, nothing):
        base = n * (8 * PITCH)
        near = pl.ds(pl.multiple_of(n * 8, 8), 8)
        deep = pl.ds(pl.multiple_of(NI + n * 8, 8), 8)
        u_below, u_above = beside((first_ref, second_ref, third_ref), near)
        k_below, k_above = beside((first_ref, second_ref, third_ref), deep)

        def tile(ref, j):
            return ref[pl.ds(base + j, 8, stride=PITCH), :]

        u, k = tile(u_ref, 0), tile(k_ref, 0)
        _, d_before = slope(u_below)
        flux_before = (k + k_below) * (u - u_below)
        ahead, d = slope(u)
        for j in range(NJ):
            if j < NJ - 1:
                u_next, k_next = tile(u_ref, j + 1), tile(k_ref, j + 1)
            else:
                u_next, k_next = u_above, k_above
            ahead_next, d_next = slope(u_next)
            flux = (k + k_next) * (u_next - u)
            across = tile(sum_ref, j) * (ahead - u)
            before = jnp.where(first_lane, k * u, pltpu.roll(across, 1, 1))
            f_ref[pl.ds(base + j, 8, stride=PITCH), :] = (
                u
                + (0.5 * ratio_y) * (flux - flux_before)
                + (0.5 * ratio_z) * (across - before)
                + (ratio_mix * tile(skew_ref, j)) * (d_next - d_before)
            )
            u, k, ahead, flux_before, d_before, d = u_next, k_next, ahead_next, flux, d, d_next
        return nothing

    lax.fori_loop(0, NI // 8, some, 0)


def sweep_kernel(
    f0_ref, col_ref, skew_col_ref, got_ref, t_ref, q_ref, r_ref, plane_ref,
    f_out, b_ref, send_ref, f_ref, sems,
):
    right = lax.axis_index("gz") == 0
    lane, row = lanes(), rows()
    own, far = col_ref[...], got_ref[0:NJ, :]
    own_k, far_k = pltpu.roll(own, NI, 1), pltpu.roll(far, NI, 1)
    below = jnp.broadcast_to(got_ref[NJ : NJ + 1, :], (NJ, NK))
    above = jnp.broadcast_to(got_ref[NJ + 1 : NJ + 2, :], (NJ, NK))
    up = jnp.where(row == NJ - 1, above, pltpu.roll(far, NJ - 1, 0))
    down = jnp.where(row == 0, below, pltpu.roll(far, 1, 0))
    sign = jnp.where(right, ratio_mix, -ratio_mix).astype(F32)
    extra = (0.5 * ratio_z) * (own_k * far + far_k * (far - own)) + (
        sign * skew_col_ref[...]
    ) * (up - down)
    edge = lane == jnp.where(right, NK - 1, 0)
    turn = jnp.where(right, NK - 1, NK)

    def layer(i, state):
        s, total = state
        at = pl.ds(pl.multiple_of(i * NJ, NJ), NJ)
        here = pltpu.roll(extra, (turn - i) & (NK - 1), 1)
        f = f0_ref[pl.ds(pl.multiple_of(i * PITCH, 8), NJ), :] + jnp.where(edge, here, 0.0)
        f_ref[at, :] = f
        s = f + s
        b_ref[at, :] = r_ref[at, :] * s
        total = total + q_ref[at, :] * s
        return t_ref[at, :] * s, total, s

    def leave(n):
        at = pl.ds(pl.multiple_of(n * PART, PART), PART)
        return pltpu.make_async_copy(f_ref.at[at, :], f_out.at[at, :], sems.at[n])

    def some(n, state):
        carried, total, s = state
        for m in range(PART // NJ):
            carried, total, s = layer(n * (PART // NJ) + m, (carried, total))
        leave(n).start()
        return carried, total, s

    zero = jnp.zeros((NJ, NK), F32)
    state = (zero, zero, zero)
    for n in range(ROWS // PART):
        state = some(n, state)
    _, total, s = state
    planes = [plane_ref[c * NJ : c * NJ + NJ, :] for c in range(5)] + [total, s]
    for c, plane in enumerate(planes):
        for q in range(BLOCKS):
            send_ref[q, :, c * NK : c * NK + NK] = plane[2 * q : 2 * q + 2]
    for n in range(ROWS // PART):
        leave(n).wait()


def separator_kernel(got_ref, out_ref):
    half = 0.5 * ratio_x

    def plane(p, c):
        return got_ref[p, :, c * NK : c * NK + NK]

    def inner(p):
        return plane(p, 1)

    def link(p):
        return half * (plane(p, 4) + plane(p + 1, 3))

    middle = BLOCKS // 2
    left, right = [], []
    ground = plane(0, 0) + half * plane(0, 3)
    side = plane(0, 5)
    ground_r = plane(BLOCKS - 1, 2) + half * plane(BLOCKS - 1, 4)
    side_r = plane(BLOCKS - 1, 6)
    for m in range(middle):
        p, o = m, BLOCKS - 1 - m
        r = 1.0 / (ground + inner(p))
        t = inner(p) * r
        left.append((side * r, t))
        ground, side = plane(p, 2) + t * ground, plane(p, 6) + t * side
        r = 1.0 / (ground_r + inner(o))
        t = inner(o) * r
        right.append((side_r * r, t))
        ground_r, side_r = plane(o, 0) + t * ground_r, plane(o, 5) + t * side_r
        if m < middle - 1:
            r = 1.0 / (ground + link(p))
            t = link(p) * r
            left.append((side * r, t))
            ground, side = plane(p + 1, 0) + t * ground, plane(p + 1, 5) + t * side
            r = 1.0 / (ground_r + link(o - 1))
            t = link(o - 1) * r
            right.append((side_r * r, t))
            ground_r, side_r = plane(o - 1, 2) + t * ground_r, plane(o - 1, 6) + t * side_r
    joint = link(middle - 1)
    r = 1.0 / (ground + joint)
    t = joint * r
    left.append((side * r, t))
    value = (side_r + t * side) / (ground_r + t * ground)
    there = value
    values_r = [there]
    for b, t in reversed(right):
        there = b + t * there
        values_r.append(there)
    here = value
    values_l = []
    for b, t in reversed(left):
        here = b + t * here
        values_l.append(here)
    values = values_l[::-1] + values_r
    for n, v in enumerate(values):
        out_ref[2 * n : 2 * n + 2, :] = v


def back_kernel(v_ref, b_ref, t_ref, q_ref, w_out, w_ref, sems):
    half = NJ // 2
    for c in range(4):
        w_ref[pl.ds(c // 2 * NJ + c % 2, half, stride=2), :] = v_ref[pl.ds(c, half, stride=4), :]
    head, tail = w_ref[0:NJ, :], w_ref[NJ : 2 * NJ, :]

    def layer(i, w):
        at = pl.ds(i * NJ, NJ)
        w = (b_ref[at, :] + q_ref[at, :] * head) + t_ref[at, :] * w
        w_ref[at, :] = w
        return w

    w_ref[ROWS - NJ : ROWS, :] = tail
    w = tail
    copies = []
    for n in reversed(range(ROWS // PART)):
        for i in reversed(range(n * (PART // NJ), min((n + 1) * (PART // NJ), NI - 1))):
            w = layer(i, w)
        at = pl.ds(n * PART, PART)
        copies.append(pltpu.make_async_copy(w_ref.at[at, :], w_out.at[at, :], sems.at[n]))
        copies[-1].start()
    for copy in copies:
        copy.wait()


def body(initial_thermal_state, thermal_spread_rate, yz_skew_factor):
    u = initial_thermal_state.reshape(ROWS, NK)
    k = thermal_spread_rate.reshape(ROWS, NK)
    block = ROWS * NK
    single = (NI, NJ, 1, NK)
    anywhere = pl.BlockSpec(memory_space=pltpu.HBM)
    whole = pl.BlockSpec(memory_space=pltpu.VMEM)
    sent = pl.pallas_call(
        edge_kernel,
        out_shape=[pltpu.VMEM((2 * NI, NK), F32)] * 3,
        in_specs=[anywhere] * 2,
        out_specs=[whole] * 3,
        scratch_shapes=[pltpu.SemaphoreType.DMA((6,))],
        compiler_params=pltpu.CompilerParams(vmem_limit_bytes=56 * 1024 * 1024),
        cost_estimate=pl.CostEstimate(flops=0, bytes_accessed=8 * NI * NK * 4, transcendentals=0),
        name="edges",
    )(initial_thermal_state.reshape(single), thermal_spread_rate.reshape(single))
    count = lax.axis_size("gy")
    run = count // 2
    swaps = (
        [(i, i + 1) for i in (*range(1, run - 1, 2), *range(run, count, 2))],
        [(i, i + 1) for i in (*range(0, run - 2, 2), *range(run - 1, count - 1, 2))],
        [(run - 2, run - 1)],
    )
    beyond = [
        lax.ppermute(rows, "gy", [way for a, b in pairs for way in ((a, b), (b, a))])
        for rows, pairs in zip(sent, swaps)
    ]
    spread = (NI * PITCH, NK)
    col, u_wide, k_wide, k_sum = call(
        pack_kernel, [(NJ, NK)] + [spread] * 3, 2, 6 * block, 20 * block, "pack"
    )(u, k)
    t, q, r, planes, skew, skew_col = call(
        factor_kernel, [(ROWS, NK)] * 3 + [(5 * NJ, NK), spread, (NJ, NK)], 2, 20 * block, 22 * block, "factor"
    )(k, yz_skew_factor)
    (to_half,) = call(corner_kernel, [(NJ + 8, NK)], 4, NI * NK, 0, "corner")(*beyond, col)
    got_col = lax.ppermute(to_half, "gz", [(0, 1), (1, 0)])
    (f0,) = call(source_kernel, [spread], 7, 40 * block, 16 * block, "source")(
        u_wide, k_wide, k_sum, skew, *beyond
    )
    f, b, send = call(
        sweep_kernel, [(ROWS, NK)] * 2 + [(BLOCKS, 2, PLANES * NK)], 8,
        8 * block, 24 * block, "sweep", True,
    )(f0, col, skew_col, got_col, t, q, r, planes)
    got = lax.all_to_all(send, "gx", 0, 0, tiled=True)
    (values,) = call(
        separator_kernel, [(4 * BLOCKS, NK)], 1, block, block, "separator"
    )(got)
    mine = lax.all_to_all(values, "gx", 0, 0, tiled=True)
    (w,) = call(back_kernel, [(ROWS, NK)], 4, 4 * block, 16 * block, "back", True)(mine, b, t, q)
    shape = initial_thermal_state.shape
    return f.reshape(shape), w.reshape(shape)


def solution(mesh):
    spec = P("gx", "gy", "gz")
    return jax.shard_map(
        body, mesh=mesh, in_specs=(spec, spec, spec), out_specs=(spec, spec), check_vma=False
    )
```
